32 devices in a mesh: seq: 16 (over z, x, core), chan: 2 (over y).
Axes of the slice: x: 2, y: 2, z: 4, core: 2. Of those that a mesh axis runs over, the one named last changes fastest.
Arguments:
- features: bfloat16 [4096, 3, 8192], P('seq', None, 'chan'), may hold values from -6 to 6
- residual_in: bfloat16 [4096, 8192], P('seq', 'chan'), may hold values from -6 to 6
- short_filter: float32 [3, 3, 8192], P(None, None, 'chan'), may hold values from -3.5 to 3.5
- decay_rates: float32 [8192, 16], P('chan'), as said below
- residues: float32 [8192, 16], P('chan'), may hold values from -0.12 to 0.12
- skip_gain: float32 [8192], P('chan'), may hold values from -4 to 4
- out_weight: bfloat16 [8192, 8192], P('chan', 'seq'), may hold values from -0.09375 to 0.09375
- final_gain: float32 [8192], P('chan'), may hold values from 0.5 to 1.5
- embedding: bfloat16 [512, 8192], P(None, 'chan')
- next_ids: int32 [4096], P('seq'), may hold values from 65 to 84, as said below
Outputs:
- block_out: bfloat16 [4096, 8192], P('seq', 'chan')
- log_like: float32 [4096], P('seq')
The draws below stay inside these ranges and needn't reach their ends.
Inputs may be any that keep to these rules, and one draw needn't show every extreme that they name: `next_ids`: each entry is one of 65, 67, 71, 84. `decay_rates`: all between 1.2e-5 and 0.05.
All inputs are finite; a program needn't handle non-finite values.
Results may differ from the reference program's by a relative error of at most 0.015.
Values may be sent and summed in bfloat16 or wider, within the bound.
No kernel may reach another device: no remote copies, remote signals or barrier semaphores. Data moves between devices by JAX's collectives and lax.ppermute only.
A program may use at most 256 MiB of HBM per device.

```python
import math
import jax
import jax.numpy as jnp
from jax import lax

D = 8192
VOCAB = 512
SHORT = 3
STATE = 16
TOKENS = 4096


def draw_decay_rates(key, part):
    key = jax.random.fold_in(key, 11)
    lowest = 0.3 / TOKENS
    highest = 0.05
    unit = jax.random.uniform(key, (D, STATE), jnp.float32)
    return jnp.exp(math.log(lowest) + unit * (math.log(highest) - math.log(lowest)))


def draw_embedding(key, part):
    key = jax.random.fold_in(key, 12)
    first_key, second_key = jax.random.split(key, 2)
    scales = jnp.exp(jax.random.uniform(second_key, (VOCAB, 1), jnp.float32) * math.log(1.25))
    basis = jax.random.normal(first_key, (VOCAB, D), jnp.float32) * (3.0 / math.sqrt(D))
    table = basis * scales
    return table.astype(jnp.bfloat16)


def draw_next_ids(key, part):
    key = jax.random.fold_in(key, 13)
    letter = jax.random.randint(key, (TOKENS,), 0, 4)
    alphabet = jnp.array([65, 67, 71, 84], dtype=jnp.int32)
    return alphabet[letter]


def raised(result, key, source, target, parts, factor):
    owner, partner = [(jnp.arange(result.shape[position]) // (result.shape[position] // parts)).reshape([-1 if axis == position else 1 for axis in range(result.ndim)]) for position in (source, target)]
    chosen = jax.random.permutation(key, parts)[partner]
    strong = (owner == chosen) | (owner == (partner + parts // 2) % parts)
    return jnp.where(strong, factor * result, result)


def shard_levels(own_key, dims, shards, least, high):
    factor_of = 1.0
    for axis_at, parts in shards:
        steps = jax.random.uniform(jax.random.fold_in(jax.random.fold_in(own_key, 6), axis_at), (parts,), jnp.float32, least / len(shards), high / len(shards))
        factor_of = factor_of * jnp.repeat(jnp.exp(steps), dims[axis_at] // parts).reshape((-1,) + (1,) * (len(dims) - 1 - axis_at))
    return factor_of


def centred(own_key, extent, scale, limit, shards=(), held_as=jnp.bfloat16):
    entries = scale * jax.random.normal(own_key, extent, jnp.float32)
    if shards:
        entries = entries * shard_levels(own_key, extent, shards, -0.22, 0.18)
    return jnp.clip(entries, -limit, limit).astype(held_as)


def gaussian_with(stream_key, dims, spread, most, cuts, heavy, kind=jnp.bfloat16):
    drawn = spread * jax.random.normal(stream_key, dims, jnp.float32)
    if cuts:
        drawn = drawn * shard_levels(stream_key, dims, cuts, -0.22, 0.18)
    return jnp.clip(raised(drawn, jax.random.fold_in(stream_key, 3), *heavy), -most, most).astype(kind)


def setup_inputs(seed: int = 0) -> dict:
    arg_keys = jax.random.split(jax.random.key(seed), 11)
    return {
        "features": centred(arg_keys[0], (TOKENS, 3, D), 1.0, 6.0, ((0, 16), (2, 2))),
        "residual_in": centred(arg_keys[1], (TOKENS, D), 1.0, 6.0, ((0, 16), (1, 2))),
        "short_filter": centred(arg_keys[2], (SHORT, 3, D), SHORT ** -0.5, 3.5, ((2, 2),), jnp.float32),
        "decay_rates": draw_decay_rates(jax.random.fold_in(arg_keys[10], 71), 0),
        "residues": centred(arg_keys[4], (D, STATE), 0.02, 0.12, ((0, 2),), jnp.float32),
        "skip_gain": centred(arg_keys[5], (D,), 1.0, 4.0, ((0, 2),), jnp.float32),
        "out_weight": gaussian_with(arg_keys[6], (D, D), D ** -0.5, 0.09375, ((0, 2), (1, 16)), (0, 1, 16, 2.0)),
        "final_gain": jnp.clip(1.0 + 0.1 * jax.random.normal(arg_keys[7], (D,), jnp.float32), 0.5, 1.5),
        "embedding": draw_embedding(jax.random.fold_in(arg_keys[10], 71), 0),
        "next_ids": draw_next_ids(jax.random.fold_in(arg_keys[10], 71), 0),
    }


def long_block(inputs):
    signal, rates_part, residue_part = inputs
    offsets = jnp.arange(TOKENS, dtype=jnp.float32)
    kernel = jnp.einsum('cm,cmt->ct', residue_part, jnp.exp(-rates_part[:, :, None] * offsets[None, None, :]), precision=lax.Precision.HIGHEST)
    length = 2 * TOKENS
    product = jnp.fft.rfft(signal, n=length) * jnp.fft.rfft(kernel, n=length)
    return jnp.fft.irfft(product, n=length)[:, :TOKENS]

def reference(features, residual_in, short_filter, decay_rates, residues, skip_gain, out_weight, final_gain, embedding, next_ids):
    streams = features.astype(jnp.float32)
    padded = jnp.pad(streams, ((SHORT - 1, 0), (0, 0), (0, 0)))
    short = short_filter[0] * padded[SHORT - 1:SHORT - 1 + TOKENS]
    for offset in range(1, SHORT):
        short = short + short_filter[offset] * padded[SHORT - 1 - offset:SHORT - 1 - offset + TOKENS]
    queries = short[:, 0, :]
    mixed_kv = (short[:, 1, :] * short[:, 2, :]).astype(jnp.bfloat16)
    group_size = min(128, D)
    groups = D // group_size
    signal = mixed_kv.astype(jnp.float32).T.reshape(groups, group_size, TOKENS)
    rates_grouped = decay_rates.reshape(groups, group_size, STATE)
    residue_grouped = residues.reshape(groups, group_size, STATE)
    convolved = lax.map(long_block, (signal, rates_grouped, residue_grouped))
    filtered = convolved.reshape(D, TOKENS).T.astype(jnp.bfloat16)
    gated = (queries * (filtered.astype(jnp.float32) + skip_gain * mixed_kv.astype(jnp.float32))).astype(jnp.bfloat16)
    projected = jnp.dot(gated, out_weight, preferred_element_type=jnp.float32)
    block_out = (residual_in.astype(jnp.float32) + projected).astype(jnp.bfloat16)
    block_f = block_out.astype(jnp.float32)
    inv_rms = lax.rsqrt(lax.optimization_barrier(jnp.mean(block_f * block_f, axis=1)) + 1e-06)
    scaled = (block_f * final_gain).astype(jnp.bfloat16)
    raw_logits = lax.dot_general(scaled, embedding, (((1,), (1,)), ((), ())), preferred_element_type=jnp.float32)
    logits = raw_logits * inv_rms[:, None]
    chosen = jnp.take_along_axis(logits, next_ids[:, None].astype(jnp.int32), axis=1)[:, 0]
    log_like = chosen - jax.nn.logsumexp(logits, axis=1)
    return (block_out, log_like)
```

```python
import functools
import itertools

import jax
import jax.numpy as jnp
from jax import lax
from jax.experimental import pallas as pl
from jax.experimental.pallas import tpu as pltpu
from jax.sharding import PartitionSpec as P

F32 = jnp.float32
BF16 = jnp.bfloat16
LANES = 128
SUBLANES = 8
GROUP = LANES * SUBLANES


def xor_permute(value, axis, mask):
    count = lax.axis_size(axis)
    return lax.ppermute(value, axis, [(source, source ^ mask) for source in range(count)])


def shifted(value, axis, steps):
    count = lax.axis_size(axis)
    first, last = (max(0, -steps), min(count, count - steps))
    return lax.ppermute(value, axis, [(source, source + steps) for source in range(first, last)])


def fill_stream(scratch, halo, block):
    scratch[:SUBLANES, :] = halo
    scratch[SUBLANES:, :] = block.astype(F32)


def short_stream(scratch, taps_ref, stream, lanes, rows):
    taps = taps_ref.shape[0] // 3
    total = taps_ref[stream : stream + 1, lanes] * scratch[SUBLANES : SUBLANES + rows, lanes]
    for offset in range(1, taps):
        row = offset * 3 + stream
        start = SUBLANES - offset
        total = total + taps_ref[row : row + 1, lanes] * scratch[start : start + rows, lanes]
    return total


def lane_blocks():
    return [(part, slice(part * LANES, (part + 1) * LANES)) for part in range(SUBLANES)]


def states_kernel(
    keys_ref, values_ref, halo_ref, taps_ref, rates_ref, mixed_ref, end_ref, keys_f, values_f, rows_f
):
    rows = mixed_ref.shape[0]
    modes = rates_ref.shape[0]
    fill_stream(keys_f, halo_ref[1], keys_ref[0])
    fill_stream(values_f, halo_ref[2], values_ref[0])
    for part, lanes in lane_blocks():
        mixed = (
            short_stream(keys_f, taps_ref, 1, lanes, rows)
            * short_stream(values_f, taps_ref, 2, lanes, rows)
        ).astype(BF16)
        mixed_ref[:, lanes] = mixed
        rows_f[:, part * SUBLANES : (part + 1) * SUBLANES, :] = mixed.astype(F32).reshape(
            rows // SUBLANES, SUBLANES, LANES
        )
    decay = [jnp.exp(-rates_ref[mode]) for mode in range(modes)]

    def eight(block, states):
        for step in range(SUBLANES):
            entry = rows_f[block, pl.ds(step, SUBLANES, stride=SUBLANES), :]
            states = tuple(d * s + entry for d, s in zip(decay, states))
        return states

    zeros = tuple(jnp.zeros((SUBLANES, LANES), F32) for _ in range(modes))
    states = lax.fori_loop(0, rows // SUBLANES, eight, zeros)
    for mode in range(modes):
        end_ref[mode] = states[mode]


def gated_kernel(
    queries_ref,
    halo_ref,
    taps_ref,
    mixed_ref,
    skip_ref,
    rates_ref,
    residues_ref,
    enter_ref,
    gated_ref,
    queries_f,
    rows_f,
    long_f,
):
    rows = mixed_ref.shape[0]
    modes = rates_ref.shape[0]
    fill_stream(queries_f, halo_ref[0], queries_ref[0])
    for part, lanes in lane_blocks():
        rows_f[:, part * SUBLANES : (part + 1) * SUBLANES, :] = (
            mixed_ref[:, lanes].astype(F32).reshape(rows // SUBLANES, SUBLANES, LANES)
        )
    decay = [jnp.exp(-rates_ref[mode]) for mode in range(modes)]
    weight = [residues_ref[mode] for mode in range(modes)]

    def eight(block, states):
        for step in range(SUBLANES):
            entry = rows_f[block, pl.ds(step, SUBLANES, stride=SUBLANES), :]
            states = tuple(d * s + entry for d, s in zip(decay, states))
            terms = [w * s for w, s in zip(weight, states)]
            while len(terms) > 1:
                terms = [sum(terms[at : at + 2][1:], terms[at]) for at in range(0, len(terms), 2)]
            long_f[block, pl.ds(step, SUBLANES, stride=SUBLANES), :] = terms[0]
        return states

    lax.fori_loop(0, rows // SUBLANES, eight, tuple(enter_ref[mode] for mode in range(modes)))
    for part, lanes in lane_blocks():
        filtered = long_f[:, part * SUBLANES : (part + 1) * SUBLANES, :].reshape(rows, LANES)
        filtered = filtered.astype(BF16).astype(F32)
        direct = skip_ref[:, lanes] * mixed_ref[:, lanes].astype(F32)
        queries = short_stream(queries_f, taps_ref, 0, lanes, rows)
        gated_ref[:, lanes] = (queries * (filtered + direct)).astype(BF16)


def vmem_params(mib):
    return pltpu.CompilerParams(
        dimension_semantics=("arbitrary",), vmem_limit_bytes=mib * 1024 * 1024
    )


def mixed_and_states(streams, halo, taps, rates):
    rows, width = streams.shape[1:]
    modes = rates.shape[0]
    stream = lambda which: pl.BlockSpec((1, rows, GROUP), lambda g: (which, 0, g))
    modal = pl.BlockSpec((modes, SUBLANES, LANES), lambda g: (0, g, 0))
    return pl.pallas_call(
        states_kernel,
        grid=(width // GROUP,),
        in_specs=[
            stream(1),
            stream(2),
            pl.BlockSpec((3, SUBLANES, GROUP), lambda g: (0, 0, g)),
            pl.BlockSpec((taps.shape[0], GROUP), lambda g: (0, g)),
            modal,
        ],
        out_specs=[pl.BlockSpec((rows, GROUP), lambda g: (0, g)), modal],
        out_shape=[
            jax.ShapeDtypeStruct((rows, width), BF16),
            jax.ShapeDtypeStruct(rates.shape, F32),
        ],
        scratch_shapes=[
            pltpu.VMEM((rows + SUBLANES, GROUP), F32),
            pltpu.VMEM((rows + SUBLANES, GROUP), F32),
            pltpu.VMEM((rows // SUBLANES, SUBLANES * SUBLANES, LANES), F32),
        ],
        compiler_params=vmem_params(32),
        cost_estimate=pl.CostEstimate(flops=rows * width, bytes_accessed=rows, transcendentals=0),
        name="mixed_and_states",
    )(streams, streams, halo, taps, rates)


def gated_rows(streams, halo, taps, mixed, skip, rates, residues, entering, base, steps):
    rows, width = mixed.shape
    modes = rates.shape[0]
    modal = pl.BlockSpec((modes, SUBLANES, LANES), lambda g: (0, base + g, 0))
    return pl.pallas_call(
        gated_kernel,
        grid=(steps,),
        in_specs=[
            pl.BlockSpec((1, rows, GROUP), lambda g: (0, 0, base + g)),
            pl.BlockSpec((3, SUBLANES, GROUP), lambda g: (0, 0, base + g)),
            pl.BlockSpec((taps.shape[0], GROUP), lambda g: (0, base + g)),
            pl.BlockSpec((rows, GROUP), lambda g: (0, base + g)),
            pl.BlockSpec((1, GROUP), lambda g: (0, base + g)),
            modal,
            modal,
            modal,
        ],
        out_specs=pl.BlockSpec((rows, GROUP), lambda g: (0, g)),
        out_shape=jax.ShapeDtypeStruct((rows, steps * GROUP), BF16),
        scratch_shapes=[
            pltpu.VMEM((rows + SUBLANES, GROUP), F32),
            pltpu.VMEM((rows // SUBLANES, SUBLANES * SUBLANES, LANES), F32),
            pltpu.VMEM((rows // SUBLANES, SUBLANES * SUBLANES, LANES), F32),
        ],
        compiler_params=vmem_params(32),
        cost_estimate=pl.CostEstimate(flops=rows * width, bytes_accessed=rows, transcendentals=0),
        name="gated_rows",
    )(streams, halo, taps, mixed, skip, rates, residues, entering)


def entering_states(end, rates, rows, merges, before_last=()):
    place = lax.axis_index("seq")
    total, entering = end, jnp.zeros_like(end)
    held = []
    for bits in merges:
        span, count = 1 << bits[0], 1 << len(bits)
        last = bits == merges[-1]
        if last and before_last:
            total, *held = tied(total, *before_last)
        extra = span >> 1 if last and count == 2 else 0
        others = [
            (mask, xor_permute(total, "seq", (mask * span) | extra)) for mask in range(1, count)
        ]
        own = (place // span) % count
        inside = (place % span) * rows
        merged = jnp.zeros_like(total)
        for mask, value in [(0, total), *others]:
            run = own ^ mask
            gap = jnp.maximum(own - 1 - run, 0) * (span * rows) + inside
            ahead = jnp.exp(-rates * gap.astype(F32)) * value
            entering = entering + jnp.where(run < own, ahead, 0.0)
            gap = (count - 1 - run) * (span * rows)
            merged = merged + jnp.exp(-rates * gap.astype(F32)) * value
        total = merged
    return entering, held


def output_kernel(
    order_ref, added_ref, residual_ref, gain_ref, table_ref, block_ref, packed_ref, logits, squares
):
    at = pl.program_id(0)

    @pl.when(at == 0)
    def _():
        logits[...] = jnp.zeros_like(logits)
        squares[...] = jnp.zeros_like(squares)

    block = (residual_ref[...].astype(F32) + added_ref[0].astype(F32)).astype(BF16)
    block_ref[...] = block
    block_f = block.astype(F32)
    scaled = (block_f * gain_ref[...]).astype(BF16)
    logits[...] += lax.dot_general(
        table_ref[...], scaled, (((1,), (1,)), ((), ())), preferred_element_type=F32
    )
    squared = block_f * block_f
    width = squared.shape[1]
    for start in range(0, width, LANES):
        squares[...] += squared[:, start : start + LANES]

    @pl.when(at == pl.num_programs(0) - 1)
    def _():
        vocab = logits.shape[0]
        summed = jnp.sum(squares[...].T, axis=0, keepdims=True)
        high = summed.astype(BF16).astype(F32)
        row = lax.broadcasted_iota(jnp.int32, (16, summed.shape[1]), 0)
        extra = jnp.where(row == 0, high, jnp.where(row == 1, summed - high, 0.0))
        packed_ref[:vocab, :] = logits[...].astype(BF16)
        packed_ref[vocab:, :] = extra.astype(BF16)


def output_rows(order, added, residual_in, gain, table):
    parts, rows, width = added.shape
    vocab = table.shape[0]
    return pl.pallas_call(
        output_kernel,
        grid_spec=pltpu.PrefetchScalarGridSpec(
            num_scalar_prefetch=1,
            grid=(parts,),
            in_specs=[
                pl.BlockSpec((1, rows, width), lambda p, order: (order[p], 0, 0)),
                pl.BlockSpec((rows, width), lambda p, order: (0, p)),
                pl.BlockSpec((1, width), lambda p, order: (0, p)),
                pl.BlockSpec((vocab, width), lambda p, order: (0, p)),
            ],
            out_specs=[
                pl.BlockSpec((rows, width), lambda p, order: (0, p)),
                pl.BlockSpec((vocab + 16, rows), lambda p, order: (0, 0)),
            ],
            scratch_shapes=[
                pltpu.VMEM((vocab, rows), F32),
                pltpu.VMEM((rows, LANES), F32),
            ],
        ),
        out_shape=[
            jax.ShapeDtypeStruct(residual_in.shape, BF16),
            jax.ShapeDtypeStruct((vocab + 16, rows), BF16),
        ],
        compiler_params=vmem_params(32),
        cost_estimate=pl.CostEstimate(
            flops=2 * rows * parts * width * vocab,
            bytes_accessed=2 * parts * width * (3 * rows + vocab),
            transcendentals=0,
        ),
        name="output_rows",
    )(order, added, residual_in, gain, table)


def like_kernel(width, first_ref, second_ref, ids_ref, like_ref):
    rows = ids_ref.shape[1]
    vocab = first_ref.shape[0] - 16
    total = first_ref[...].astype(F32) + second_ref[...].astype(F32)
    squares = total[vocab : vocab + 1, :] + total[vocab + 1 : vocab + 2, :]
    inv_rms = lax.rsqrt(squares / width + 1e-06)
    logits = total[:vocab, :] * inv_rms
    largest = jnp.max(logits, axis=0, keepdims=True)
    summed = jnp.sum(jnp.exp(logits - largest), axis=0, keepdims=True)
    vocab_ids = lax.broadcasted_iota(jnp.int32, (vocab, rows), 0)
    chosen = jnp.sum(jnp.where(vocab_ids == ids_ref[...], logits, 0.0), axis=0, keepdims=True)
    like_ref[...] = chosen - (largest + jnp.log(summed))


def log_likelihood(first, second, next_ids, width):
    rows = next_ids.shape[0]
    like = pl.pallas_call(
        functools.partial(like_kernel, width),
        out_shape=jax.ShapeDtypeStruct((1, rows), F32),
        compiler_params=pltpu.CompilerParams(vmem_limit_bytes=16 * 1024 * 1024),
        name="log_likelihood",
    )(first, second, next_ids[None, :])
    return like[0]


def summed_over_chan(value):
    count = lax.axis_size("chan")
    total, span = value, 1
    while span < count // 2:
        total = (total.astype(F32) + xor_permute(total, "chan", span).astype(F32)).astype(BF16)
        span *= 2
    return total, xor_permute(total, "chan", span)


def placed_pairs(count, chans, per_chan, same, seq_mask, chan_mask):
    pairs = []
    for place, chan in itertools.product(range(count), range(chans)):
        if (place // per_chan == chan) == same:
            target = (place ^ seq_mask) * chans + (chan ^ chan_mask)
            pairs.append((place * chans + chan, target))
    return pairs


def tied(*values):
    return lax.optimization_barrier(values)


def far_pieces(out_weight, cuts):
    return [
        lax.slice_in_dim(out_weight, first, last, axis=1)
        for first, last in itertools.pairwise(cuts)
    ]


def joined(*rows):
    return tied(jnp.concatenate([jnp.concatenate(parts, axis=1) for parts in rows], axis=0))[0]


def product(rows, *weights):
    outs = [jnp.dot(rows, weight, preferred_element_type=F32).astype(BF16) for weight in weights]
    return outs[0] if len(outs) == 1 else jnp.concatenate(outs, axis=1)


def projected_fast(gated, out_weight, core_weight, far):
    count, chans = lax.axis_size("seq"), lax.axis_size("chan")
    per_chan = count // chans
    rows, block = gated[0].shape[0], out_weight.shape[1]
    core, side, low = 1, 2, 4

    below = [xor_permute(part, "seq", low) for part in gated]
    beside = [xor_permute(gated[0], "seq", side)]
    later, far[1] = tied(gated[1], far[1])
    beside.append(xor_permute(later, "seq", side))
    below[0], beside[1] = tied(below[0], beside[1])
    across = [xor_permute(below[0], "seq", side)]
    beside[0], far[2], far[0] = tied(beside[0], far[2], far[0])
    first = joined(gated, beside)
    near_first = product(first, out_weight, core_weight)
    below[1], across[0], waiting = tied(below[1], across[0], far[3])
    far[3] = xor_permute(waiting, "seq", per_chan)
    across.append(xor_permute(below[1], "seq", side))
    second = joined(below, across)

    def reduced(partial, masks, same, after=None):
        pairs = placed_pairs(count, chans, per_chan, not same, 0, 1)
        other = lax.ppermute(partial, ("seq", "chan"), pairs)
        if after is not None:
            other, _ = tied(other, after)
        total = (partial.astype(F32) + other.astype(F32)).astype(BF16)
        back = []
        for at, mask in enumerate(masks):
            mine = total[at * rows : (at + 1) * rows]
            if mask:
                pairs = placed_pairs(count, chans, per_chan, same, mask, 0)
                mine = lax.ppermute(mine, ("seq", "chan"), pairs)
            back.append(mine)
        return back

    far_core = [xor_permute(piece, "seq", core) for piece in far[:-1]]
    near_back = reduced(near_first, (0, side), True)
    early = jnp.concatenate(far[:-1] + far_core, axis=1)
    early_first = product(first, early)
    near_second = product(second, out_weight, core_weight)
    early_second = product(second, early)
    last, *_ = tied(far[-1], early_second, near_second)
    last_core = xor_permute(last, "seq", core)
    last = jnp.concatenate([last, last_core], axis=1)
    last_all = jnp.concatenate([product(first, last), product(second, last)], axis=0)
    near_back += reduced(near_second, (low, low | side), True, last_all)
    early_back = reduced(early_first, (0, side), False)
    early_back += reduced(early_second, (low, low | side), False, last_all)
    last_back = reduced(last_all, (0, side, low, low | side), False)
    here = lax.axis_index("seq") // per_chan == lax.axis_index("chan")
    cut = block - last_core.shape[1]
    blocks = {}
    for at, mask in enumerate((0, side, low, low | side)):
        for half in range(2):
            near_block = near_back[at][:, half * block : (half + 1) * block]
            late_block = jnp.concatenate(
                [
                    early_back[at][:, half * cut : (half + 1) * cut],
                    last_back[at][:, half * (block - cut) : (half + 1) * (block - cut)],
                ],
                axis=1,
            )
            blocks[mask | (half * core)] = jnp.where(here, near_block, late_block)
    added = jnp.stack([blocks[mask] for mask in range(per_chan)])
    order = jnp.arange(per_chan, dtype=jnp.int32) ^ (lax.axis_index("seq") % per_chan)
    return added, order


def projected_plain(gated, out_weight):
    count, chans = lax.axis_size("seq"), lax.axis_size("chan")
    per_chan = count // chans
    partial = jnp.dot(
        gated,
        lax.all_gather(out_weight, "seq", axis=1, tiled=True),
        preferred_element_type=F32,
    )
    summed = lax.psum_scatter(partial, "chan", scatter_dimension=1, tiled=True)
    rows = gated.shape[0]
    added = summed.reshape(rows, per_chan, -1).transpose(1, 0, 2)
    return added, jnp.arange(per_chan, dtype=jnp.int32)


def local(
    features,
    residual_in,
    short_filter,
    decay_rates,
    residues,
    skip_gain,
    out_weight,
    final_gain,
    embedding,
    next_ids,
):
    rows, _, width = features.shape
    short_len = short_filter.shape[0]
    modes = decay_rates.shape[1]
    streams = jnp.transpose(features, (1, 0, 2))
    rim = shifted(features[rows - (short_len - 1) :], "seq", 1)
    halo = jnp.pad(
        jnp.transpose(rim, (1, 0, 2)).astype(F32), ((0, 0), (SUBLANES - (short_len - 1), 0), (0, 0))
    )
    taps = short_filter.reshape(short_len * 3, width)
    rates = decay_rates.T.reshape(modes, width // LANES, LANES)
    weights = residues.T.reshape(modes, width // LANES, LANES)
    count, chans = lax.axis_size("seq"), lax.axis_size("chan")
    fast = chans == 2 and count == 16
    top = count // chans
    if fast:
        block = out_weight.shape[1]
        far = far_pieces(out_weight, range(0, block + 1, block // 4))
        far = [xor_permute(piece, "seq", top) for piece in far[:3]] + far[3:]
        core_weight = xor_permute(out_weight, "seq", 1)

    mixed, end = mixed_and_states(streams, halo, taps, rates)
    bits = range(count.bit_length() - 1)
    merges = [(0,), (1, 2), (3,)] if fast else [(bit,) for bit in bits]
    entering, held = entering_states(end, rates, rows, merges, far[:1] if fast else ())
    if fast:
        far = held + far[1:]
    if fast:
        entering, core_weight = tied(entering, core_weight)
    groups = width // GROUP
    edges = (0, groups // 2, groups) if fast else (0, groups)
    gated = []
    for base, stop in itertools.pairwise(edges):
        gated.append(
            gated_rows(
                streams,
                halo,
                taps,
                mixed,
                skip_gain[None, :],
                rates,
                weights,
                entering,
                base,
                stop - base,
            )
        )
        entering, _ = tied(entering, gated[-1])
    if fast:
        added, order = projected_fast(gated, out_weight, core_weight, far)
    else:
        added, order = projected_plain(gated[0], out_weight)
    block_out, packed = output_rows(order, added, residual_in, final_gain[None, :], embedding)
    first, second = summed_over_chan(packed)
    return block_out, log_likelihood(first, second, next_ids, float(width * chans))


def solution(mesh):
    return jax.shard_map(
        local,
        mesh=mesh,
        in_specs=(
            P("seq", None, "chan"),
            P("seq", "chan"),
            P(None, None, "chan"),
            P("chan", None),
            P("chan", None),
            P("chan"),
            P("chan", "seq"),
            P("chan"),
            P(None, "chan"),
            P("seq"),
        ),
        out_specs=(P("seq", "chan"), P("seq")),
        check_vma=False,
    )
```

```python
import functools
import itertools

import jax
import jax.numpy as jnp
from jax import lax
from jax.experimental import pallas as pl
from jax.experimental.pallas import tpu as pltpu
from jax.sharding import PartitionSpec as P

F32 = jnp.float32
BF16 = jnp.bfloat16
LANES = 128
SUBLANES = 8
GROUP = LANES * SUBLANES


def xor_permute(value, axis, mask):
    count = lax.axis_size(axis)
    return lax.ppermute(value, axis, [(source, source ^ mask) for source in range(count)])


def shifted(value, axis, steps):
    count = lax.axis_size(axis)
    first, last = (max(0, -steps), min(count, count - steps))
    return lax.ppermute(value, axis, [(source, source + steps) for source in range(first, last)])


def fill_stream(scratch, halo, block):
    scratch[:SUBLANES, :] = halo
    scratch[SUBLANES:, :] = block.astype(F32)


def short_stream(scratch, taps_ref, stream, lanes, rows):
    taps = taps_ref.shape[0] // 3
    total = taps_ref[stream : stream + 1, lanes] * scratch[SUBLANES : SUBLANES + rows, lanes]
    for offset in range(1, taps):
        row = offset * 3 + stream
        start = SUBLANES - offset
        total = total + taps_ref[row : row + 1, lanes] * scratch[start : start + rows, lanes]
    return total


def lane_blocks():
    return [(part, slice(part * LANES, (part + 1) * LANES)) for part in range(SUBLANES)]


def states_kernel(
    keys_ref, values_ref, halo_ref, taps_ref, rates_ref, mixed_ref, end_ref, keys_f, values_f, rows_f
):
    rows = mixed_ref.shape[0]
    modes = rates_ref.shape[0]
    fill_stream(keys_f, halo_ref[1], keys_ref[0])
    fill_stream(values_f, halo_ref[2], values_ref[0])
    for part, lanes in lane_blocks():
        mixed = (
            short_stream(keys_f, taps_ref, 1, lanes, rows)
            * short_stream(values_f, taps_ref, 2, lanes, rows)
        ).astype(BF16)
        mixed_ref[:, lanes] = mixed
        rows_f[:, part * SUBLANES : (part + 1) * SUBLANES, :] = mixed.astype(F32).reshape(
            rows // SUBLANES, SUBLANES, LANES
        )
    decay = [jnp.exp(-rates_ref[mode]) for mode in range(modes)]

    def eight(block, states):
        for step in range(SUBLANES):
            entry = rows_f[block, pl.ds(step, SUBLANES, stride=SUBLANES), :]
            states = tuple(d * s + entry for d, s in zip(decay, states))
        return states

    zeros = tuple(jnp.zeros((SUBLANES, LANES), F32) for _ in range(modes))
    states = lax.fori_loop(0, rows // SUBLANES, eight, zeros)
    for mode in range(modes):
        end_ref[mode] = states[mode]


def gated_kernel(
    queries_ref,
    halo_ref,
    taps_ref,
    mixed_ref,
    skip_ref,
    rates_ref,
    residues_ref,
    enter_ref,
    gated_ref,
    queries_f,
    rows_f,
    long_f,
):
    rows = mixed_ref.shape[0]
    modes = rates_ref.shape[0]
    fill_stream(queries_f, halo_ref[0], queries_ref[0])
    for part, lanes in lane_blocks():
        rows_f[:, part * SUBLANES : (part + 1) * SUBLANES, :] = (
            mixed_ref[:, lanes].astype(F32).reshape(rows // SUBLANES, SUBLANES, LANES)
        )
    decay = [jnp.exp(-rates_ref[mode]) for mode in range(modes)]
    weight = [residues_ref[mode] for mode in range(modes)]

    def eight(block, states):
        for step in range(SUBLANES):
            entry = rows_f[block, pl.ds(step, SUBLANES, stride=SUBLANES), :]
            states = tuple(d * s + entry for d, s in zip(decay, states))
            terms = [w * s for w, s in zip(weight, states)]
            while len(terms) > 1:
                terms = [sum(terms[at : at + 2][1:], terms[at]) for at in range(0, len(terms), 2)]
            long_f[block, pl.ds(step, SUBLANES, stride=SUBLANES), :] = terms[0]
        return states

    lax.fori_loop(0, rows // SUBLANES, eight, tuple(enter_ref[mode] for mode in range(modes)))
    for part, lanes in lane_blocks():
        filtered = long_f[:, part * SUBLANES : (part + 1) * SUBLANES, :].reshape(rows, LANES)
        filtered = filtered.astype(BF16).astype(F32)
        direct = skip_ref[:, lanes] * mixed_ref[:, lanes].astype(F32)
        queries = short_stream(queries_f, taps_ref, 0, lanes, rows)
        gated_ref[:, lanes] = (queries * (filtered + direct)).astype(BF16)


def vmem_params(mib):
    return pltpu.CompilerParams(
        dimension_semantics=("arbitrary",), vmem_limit_bytes=mib * 1024 * 1024
    )


def mixed_and_states(streams, halo, taps, rates):
    rows, width = streams.shape[1:]
    modes = rates.shape[0]
    stream = lambda which: pl.BlockSpec((1, rows, GROUP), lambda g: (which, 0, g))
    modal = pl.BlockSpec((modes, SUBLANES, LANES), lambda g: (0, g, 0))
    return pl.pallas_call(
        states_kernel,
        grid=(width // GROUP,),
        in_specs=[
            stream(1),
            stream(2),
            pl.BlockSpec((3, SUBLANES, GROUP), lambda g: (0, 0, g)),
            pl.BlockSpec((taps.shape[0], GROUP), lambda g: (0, g)),
            modal,
        ],
        out_specs=[pl.BlockSpec((rows, GROUP), lambda g: (0, g)), modal],
        out_shape=[
            jax.ShapeDtypeStruct((rows, width), BF16),
            jax.ShapeDtypeStruct(rates.shape, F32),
        ],
        scratch_shapes=[
            pltpu.VMEM((rows + SUBLANES, GROUP), F32),
            pltpu.VMEM((rows + SUBLANES, GROUP), F32),
            pltpu.VMEM((rows // SUBLANES, SUBLANES * SUBLANES, LANES), F32),
        ],
        compiler_params=vmem_params(32),
        cost_estimate=pl.CostEstimate(flops=rows * width, bytes_accessed=rows, transcendentals=0),
        name="mixed_and_states",
    )(streams, streams, halo, taps, rates)


def gated_rows(streams, halo, taps, mixed, skip, rates, residues, entering, base, steps):
    rows, width = mixed.shape
    modes = rates.shape[0]
    modal = pl.BlockSpec((modes, SUBLANES, LANES), lambda g: (0, base + g, 0))
    return pl.pallas_call(
        gated_kernel,
        grid=(steps,),
        in_specs=[
            pl.BlockSpec((1, rows, GROUP), lambda g: (0, 0, base + g)),
            pl.BlockSpec((3, SUBLANES, GROUP), lambda g: (0, 0, base + g)),
            pl.BlockSpec((taps.shape[0], GROUP), lambda g: (0, base + g)),
            pl.BlockSpec((rows, GROUP), lambda g: (0, base + g)),
            pl.BlockSpec((1, GROUP), lambda g: (0, base + g)),
            modal,
            modal,
            modal,
        ],
        out_specs=pl.BlockSpec((rows, GROUP), lambda g: (0, g)),
        out_shape=jax.ShapeDtypeStruct((rows, steps * GROUP), BF16),
        scratch_shapes=[
            pltpu.VMEM((rows + SUBLANES, GROUP), F32),
            pltpu.VMEM((rows // SUBLANES, SUBLANES * SUBLANES, LANES), F32),
            pltpu.VMEM((rows // SUBLANES, SUBLANES * SUBLANES, LANES), F32),
        ],
        compiler_params=vmem_params(32),
        cost_estimate=pl.CostEstimate(flops=rows * width, bytes_accessed=rows, transcendentals=0),
        name="gated_rows",
    )(streams, halo, taps, mixed, skip, rates, residues, entering)


def entering_states(end, rates, rows, merges, before_last=()):
    place = lax.axis_index("seq")
    total, entering = end, jnp.zeros_like(end)
    held = []
    for bits in merges:
        span, count = 1 << bits[0], 1 << len(bits)
        last = bits == merges[-1]
        if last and before_last:
            total, *held = tied(total, *before_last)
        others = [
            (mask, xor_permute(total, "seq", mask * span)) for mask in range(1, count)
        ]
        own = (place // span) % count
        inside = (place % span) * rows
        merged = jnp.zeros_like(total)
        for mask, value in [(0, total), *others]:
            run = own ^ mask
            gap = jnp.maximum(own - 1 - run, 0) * (span * rows) + inside
            ahead = jnp.exp(-rates * gap.astype(F32)) * value
            entering = entering + jnp.where(run < own, ahead, 0.0)
            gap = (count - 1 - run) * (span * rows)
            merged = merged + jnp.exp(-rates * gap.astype(F32)) * value
        total = merged
    return entering, held


def output_kernel(
    order_ref, added_ref, residual_ref, gain_ref, table_ref, block_ref, packed_ref, logits, squares
):
    at = pl.program_id(0)

    @pl.when(at == 0)
    def _():
        logits[...] = jnp.zeros_like(logits)
        squares[...] = jnp.zeros_like(squares)

    block = (residual_ref[...].astype(F32) + added_ref[0].astype(F32)).astype(BF16)
    block_ref[...] = block
    block_f = block.astype(F32)
    scaled = (block_f * gain_ref[...]).astype(BF16)
    logits[...] += lax.dot_general(
        table_ref[...], scaled, (((1,), (1,)), ((), ())), preferred_element_type=F32
    )
    squared = block_f * block_f
    width = squared.shape[1]
    for start in range(0, width, LANES):
        squares[...] += squared[:, start : start + LANES]

    @pl.when(at == pl.num_programs(0) - 1)
    def _():
        vocab = logits.shape[0]
        summed = jnp.sum(squares[...].T, axis=0, keepdims=True)
        high = summed.astype(BF16).astype(F32)
        row = lax.broadcasted_iota(jnp.int32, (16, summed.shape[1]), 0)
        extra = jnp.where(row == 0, high, jnp.where(row == 1, summed - high, 0.0))
        packed_ref[:vocab, :] = logits[...].astype(BF16)
        packed_ref[vocab:, :] = extra.astype(BF16)


def output_rows(order, added, residual_in, gain, table):
    parts, rows, width = added.shape
    vocab = table.shape[0]
    return pl.pallas_call(
        output_kernel,
        grid_spec=pltpu.PrefetchScalarGridSpec(
            num_scalar_prefetch=1,
            grid=(parts,),
            in_specs=[
                pl.BlockSpec((1, rows, width), lambda p, order: (order[p], 0, 0)),
                pl.BlockSpec((rows, width), lambda p, order: (0, p)),
                pl.BlockSpec((1, width), lambda p, order: (0, p)),
                pl.BlockSpec((vocab, width), lambda p, order: (0, p)),
            ],
            out_specs=[
                pl.BlockSpec((rows, width), lambda p, order: (0, p)),
                pl.BlockSpec((vocab + 16, rows), lambda p, order: (0, 0)),
            ],
            scratch_shapes=[
                pltpu.VMEM((vocab, rows), F32),
                pltpu.VMEM((rows, LANES), F32),
            ],
        ),
        out_shape=[
            jax.ShapeDtypeStruct(residual_in.shape, BF16),
            jax.ShapeDtypeStruct((vocab + 16, rows), BF16),
        ],
        compiler_params=vmem_params(32),
        cost_estimate=pl.CostEstimate(
            flops=2 * rows * parts * width * vocab,
            bytes_accessed=2 * parts * width * (3 * rows + vocab),
            transcendentals=0,
        ),
        name="output_rows",
    )(order, added, residual_in, gain, table)


def like_kernel(width, first_ref, second_ref, ids_ref, like_ref):
    rows = ids_ref.shape[1]
    vocab = first_ref.shape[0] - 16
    total = first_ref[...].astype(F32) + second_ref[...].astype(F32)
    squares = total[vocab : vocab + 1, :] + total[vocab + 1 : vocab + 2, :]
    inv_rms = lax.rsqrt(squares / width + 1e-06)
    logits = total[:vocab, :] * inv_rms
    largest = jnp.max(logits, axis=0, keepdims=True)
    summed = jnp.sum(jnp.exp(logits - largest), axis=0, keepdims=True)
    vocab_ids = lax.broadcasted_iota(jnp.int32, (vocab, rows), 0)
    chosen = jnp.sum(jnp.where(vocab_ids == ids_ref[...], logits, 0.0), axis=0, keepdims=True)
    like_ref[...] = chosen - (largest + jnp.log(summed))


def log_likelihood(first, second, next_ids, width):
    rows = next_ids.shape[0]
    like = pl.pallas_call(
        functools.partial(like_kernel, width),
        out_shape=jax.ShapeDtypeStruct((1, rows), F32),
        compiler_params=pltpu.CompilerParams(vmem_limit_bytes=16 * 1024 * 1024),
        name="log_likelihood",
    )(first, second, next_ids[None, :])
    return like[0]


def summed_over_chan(value):
    count = lax.axis_size("chan")
    total, span = value, 1
    while span < count // 2:
        total = (total.astype(F32) + xor_permute(total, "chan", span).astype(F32)).astype(BF16)
        span *= 2
    return total, xor_permute(total, "chan", span)


def tied(*values):
    return lax.optimization_barrier(values)


def column_pieces(weight, cuts):
    return [lax.slice_in_dim(weight, first, last, axis=1) for first, last in itertools.pairwise(cuts)]


def join_kernel(steps, *refs):
    pieces, out_ref = refs[:-1], refs[-1]
    half = len(pieces) // 2
    rows = pieces[0].shape[0]
    at = pl.program_id(0)
    for held, wanted in ((pieces[:half], at < steps), (pieces[half:], at >= steps)):

        @pl.when(wanted)
        def _(held=held):
            for index, piece in enumerate(held):
                out_ref[index * rows : (index + 1) * rows, :] = piece[...]


def joined(*rows_of):
    leading, others = ([parts[half] for parts in rows_of] for half in range(2))
    rows = leading[0].shape[0]
    steps, more = leading[0].shape[1] // GROUP, others[0].shape[1] // GROUP
    return pl.pallas_call(
        functools.partial(join_kernel, steps),
        grid=(steps + more,),
        in_specs=[pl.BlockSpec((rows, GROUP), lambda g: (0, jnp.minimum(g, steps - 1)))] * len(leading)
        + [pl.BlockSpec((rows, GROUP), lambda g: (0, jnp.maximum(g - steps, 0)))] * len(others),
        out_specs=pl.BlockSpec((rows * len(leading), GROUP), lambda g: (0, g)),
        out_shape=jax.ShapeDtypeStruct((rows * len(leading), (steps + more) * GROUP), BF16),
        compiler_params=vmem_params(32),
        cost_estimate=pl.CostEstimate(flops=rows * GROUP, bytes_accessed=rows, transcendentals=0),
        name="joined",
    )(*leading, *others)


def product(rows, weight):
    return jnp.dot(rows, weight, preferred_element_type=F32).astype(BF16)


def projected_fast(gated, out_weight, core_weight, far, cuts):
    count, chans = lax.axis_size("seq"), lax.axis_size("chan")
    per_chan = count // chans
    rows = gated[0].shape[0]
    core, side, low = 1, 2, 4
    here = lax.axis_index("seq") // per_chan == lax.axis_index("chan")

    below = [xor_permute(part, "seq", low) for part in gated]
    beside = [xor_permute(part, "seq", side) for part in gated]
    below[0], beside[0] = tied(below[0], beside[0])
    across = [xor_permute(below[0], "seq", side)]
    below[1], beside[1], far[0], far[1], across[0] = tied(
        below[1], beside[1], far[0], far[1], across[0]
    )
    across.append(xor_permute(below[1], "seq", side))
    first = joined(gated, beside)
    near_first = [product(first, out_weight), product(first, core_weight)]

    def far_products(rows_all, which):
        return [product(rows_all, far[which]), product(rows_all, far_core[which])]

    def shared(near, parts, span):
        first_at, last_at = span
        close = jnp.concatenate([part[:, first_at:last_at] for part in near], axis=1)
        distant = jnp.concatenate(
            [jnp.concatenate([part[half] for part in parts], axis=1) for half in range(2)], axis=1
        )
        return jnp.where(here, distant, close), jnp.where(here, close, distant)

    def summed(sent, kept):
        other = xor_permute(sent, "chan", 1)
        return (kept.astype(F32) + other.astype(F32)).astype(BF16)

    def returned(total, masks):
        back = {}
        for at, mask in enumerate(masks):
            mine = total[at * rows : (at + 1) * rows]
            back[mask] = xor_permute(mine, "seq", mask) if mask else mine
        return back

    far_core = [xor_permute(piece, "seq", core) for piece in far[:2]]
    early = (0, cuts[2])
    parts = [far_products(first, 0), far_products(first, 1)]
    sent, kept = shared(near_first, parts, early)
    sent, *across = tied(sent, *across)
    back = returned(summed(sent, kept), (0, side))
    second = joined(below, across)
    near_second = [product(second, out_weight), product(second, core_weight)]
    parts = [far_products(second, 0), far_products(second, 1)]
    total = summed(*shared(near_second, parts, early))
    last, _ = tied(far[2], parts)
    far_core.append(xor_permute(last, "seq", core))
    last_span = (cuts[2], cuts[3])
    last_total = [
        summed(*shared(near, [far_products(rows_all, 2)], last_span))
        for near, rows_all in ((near_first, first), (near_second, second))
    ]
    back |= returned(total, (low, low | side))
    last_back = returned(last_total[0], (0, side)) | returned(last_total[1], (low, low | side))
    blocks = {}
    for mask in (0, side, low, low | side):
        for half in range(2):
            blocks[mask | (half * core)] = jnp.concatenate(
                [jnp.split(value[mask], 2, axis=1)[half] for value in (back, last_back)], axis=1
            )
    added = jnp.stack([blocks[mask] for mask in range(per_chan)])
    order = jnp.arange(per_chan, dtype=jnp.int32) ^ (lax.axis_index("seq") % per_chan)
    return added, order


def projected_plain(gated, out_weight):
    count, chans = lax.axis_size("seq"), lax.axis_size("chan")
    per_chan = count // chans
    partial = jnp.dot(
        gated,
        lax.all_gather(out_weight, "seq", axis=1, tiled=True),
        preferred_element_type=F32,
    )
    summed = lax.psum_scatter(partial, "chan", scatter_dimension=1, tiled=True)
    rows = gated.shape[0]
    added = summed.reshape(rows, per_chan, -1).transpose(1, 0, 2)
    return added, jnp.arange(per_chan, dtype=jnp.int32)


def local(
    features,
    residual_in,
    short_filter,
    decay_rates,
    residues,
    skip_gain,
    out_weight,
    final_gain,
    embedding,
    next_ids,
):
    rows, _, width = features.shape
    short_len = short_filter.shape[0]
    modes = decay_rates.shape[1]
    streams = jnp.transpose(features, (1, 0, 2))
    rim = shifted(features[rows - (short_len - 1) :], "seq", 1)
    halo = jnp.pad(
        jnp.transpose(rim, (1, 0, 2)).astype(F32), ((0, 0), (SUBLANES - (short_len - 1), 0), (0, 0))
    )
    taps = short_filter.reshape(short_len * 3, width)
    rates = decay_rates.T.reshape(modes, width // LANES, LANES)
    weights = residues.T.reshape(modes, width // LANES, LANES)
    count, chans = lax.axis_size("seq"), lax.axis_size("chan")
    fast = chans == 2 and count == 16
    top = count // chans
    if fast:
        block = out_weight.shape[1]
        cuts = (0, block // 4, block * 3 // 4, block)
        far = column_pieces(out_weight, cuts)
        far[0] = xor_permute(far[0], "seq", top)
        core_weight = xor_permute(out_weight, "seq", 1)

    mixed, end = mixed_and_states(streams, halo, taps, rates)
    bits = range(count.bit_length() - 1)
    merges = [(0,), (1, 2), (3,)] if fast else [(bit,) for bit in bits]
    entering, held = entering_states(end, rates, rows, merges, far[:1] if fast else ())
    if fast:
        entering, *waiting = tied(entering, *far[1:])
        far = held + [xor_permute(piece, "seq", top) for piece in waiting]
    if fast:
        entering, core_weight = tied(entering, core_weight)
    groups = width // GROUP
    edges = (0, groups // 2, groups) if fast else (0, groups)
    gated = []
    for base, stop in itertools.pairwise(edges):
        gated.append(
            gated_rows(
                streams,
                halo,
                taps,
                mixed,
                skip_gain[None, :],
                rates,
                weights,
                entering,
                base,
                stop - base,
            )
        )
        entering, _ = tied(entering, gated[-1])
    if fast:
        added, order = projected_fast(gated, out_weight, core_weight, far, cuts)
    else:
        added, order = projected_plain(gated[0], out_weight)
    block_out, packed = output_rows(order, added, residual_in, final_gain[None, :], embedding)
    first, second = summed_over_chan(packed)
    return block_out, log_likelihood(first, second, next_ids, float(width * chans))


def solution(mesh):
    return jax.shard_map(
        local,
        mesh=mesh,
        in_specs=(
            P("seq", None, "chan"),
            P("seq", "chan"),
            P(None, None, "chan"),
            P("chan", None),
            P("chan", None),
            P("chan"),
            P("chan", "seq"),
            P("chan"),
            P(None, "chan"),
            P("seq"),
        ),
        out_specs=(P("seq", "chan"), P("seq")),
        check_vma=False,
    )
```

```python
import functools
import itertools

import jax
import jax.numpy as jnp
from jax import lax
from jax.experimental import pallas as pl
from jax.experimental.pallas import tpu as pltpu
from jax.sharding import PartitionSpec as P

F32 = jnp.float32
BF16 = jnp.bfloat16
LANES = 128
SUBLANES = 8
GROUP = LANES * SUBLANES


def xor_permute(value, axis, mask):
    count = lax.axis_size(axis)
    return lax.ppermute(value, axis, [(source, source ^ mask) for source in range(count)])


def shifted(value, axis, steps):
    count = lax.axis_size(axis)
    first, last = (max(0, -steps), min(count, count - steps))
    return lax.ppermute(value, axis, [(source, source + steps) for source in range(first, last)])


def fill_stream(scratch, halo, block):
    scratch[:SUBLANES, :] = halo
    scratch[SUBLANES:, :] = block.astype(F32)


def short_stream(scratch, taps_ref, stream, lanes, rows):
    taps = taps_ref.shape[0] // 3
    total = taps_ref[stream : stream + 1, lanes] * scratch[SUBLANES : SUBLANES + rows, lanes]
    for offset in range(1, taps):
        row = offset * 3 + stream
        start = SUBLANES - offset
        total = total + taps_ref[row : row + 1, lanes] * scratch[start : start + rows, lanes]
    return total


def lane_blocks():
    return [(part, slice(part * LANES, (part + 1) * LANES)) for part in range(SUBLANES)]


def states_kernel(
    keys_ref, values_ref, halo_ref, taps_ref, rates_ref, mixed_ref, end_ref, keys_f, values_f, rows_f
):
    rows = mixed_ref.shape[0]
    modes = rates_ref.shape[0]
    fill_stream(keys_f, halo_ref[1], keys_ref[0])
    fill_stream(values_f, halo_ref[2], values_ref[0])
    for part, lanes in lane_blocks():
        mixed = (
            short_stream(keys_f, taps_ref, 1, lanes, rows)
            * short_stream(values_f, taps_ref, 2, lanes, rows)
        ).astype(BF16)
        mixed_ref[:, lanes] = mixed
        rows_f[:, part * SUBLANES : (part + 1) * SUBLANES, :] = mixed.astype(F32).reshape(
            rows // SUBLANES, SUBLANES, LANES
        )
    decay = [jnp.exp(-rates_ref[mode]) for mode in range(modes)]

    def eight(block, states):
        for step in range(SUBLANES):
            entry = rows_f[block, pl.ds(step, SUBLANES, stride=SUBLANES), :]
            states = tuple(d * s + entry for d, s in zip(decay, states))
        return states

    zeros = tuple(jnp.zeros((SUBLANES, LANES), F32) for _ in range(modes))
    states = lax.fori_loop(0, rows // SUBLANES, eight, zeros)
    for mode in range(modes):
        end_ref[mode] = states[mode]


def gated_kernel(
    queries_ref,
    halo_ref,
    taps_ref,
    mixed_ref,
    skip_ref,
    rates_ref,
    residues_ref,
    enter_ref,
    gated_ref,
    queries_f,
    rows_f,
    long_f,
):
    rows = mixed_ref.shape[0]
    modes = rates_ref.shape[0]
    fill_stream(queries_f, halo_ref[0], queries_ref[0])
    for part, lanes in lane_blocks():
        rows_f[:, part * SUBLANES : (part + 1) * SUBLANES, :] = (
            mixed_ref[:, lanes].astype(F32).reshape(rows // SUBLANES, SUBLANES, LANES)
        )
    decay = [jnp.exp(-rates_ref[mode]) for mode in range(modes)]
    weight = [residues_ref[mode] for mode in range(modes)]

    def eight(block, states):
        for step in range(SUBLANES):
            entry = rows_f[block, pl.ds(step, SUBLANES, stride=SUBLANES), :]
            states = tuple(d * s + entry for d, s in zip(decay, states))
            terms = [w * s for w, s in zip(weight, states)]
            while len(terms) > 1:
                terms = [sum(terms[at : at + 2][1:], terms[at]) for at in range(0, len(terms), 2)]
            long_f[block, pl.ds(step, SUBLANES, stride=SUBLANES), :] = terms[0]
        return states

    lax.fori_loop(0, rows // SUBLANES, eight, tuple(enter_ref[mode] for mode in range(modes)))
    for part, lanes in lane_blocks():
        filtered = long_f[:, part * SUBLANES : (part + 1) * SUBLANES, :].reshape(rows, LANES)
        filtered = filtered.astype(BF16).astype(F32)
        direct = skip_ref[:, lanes] * mixed_ref[:, lanes].astype(F32)
        queries = short_stream(queries_f, taps_ref, 0, lanes, rows)
        gated_ref[:, lanes] = (queries * (filtered + direct)).astype(BF16)


def vmem_params(mib):
    return pltpu.CompilerParams(
        dimension_semantics=("arbitrary",), vmem_limit_bytes=mib * 1024 * 1024
    )


def mixed_and_states(streams, halo, taps, rates):
    rows, width = streams.shape[1:]
    modes = rates.shape[0]
    stream = lambda which: pl.BlockSpec((1, rows, GROUP), lambda g: (which, 0, g))
    modal = pl.BlockSpec((modes, SUBLANES, LANES), lambda g: (0, g, 0))
    return pl.pallas_call(
        states_kernel,
        grid=(width // GROUP,),
        in_specs=[
            stream(1),
            stream(2),
            pl.BlockSpec((3, SUBLANES, GROUP), lambda g: (0, 0, g)),
            pl.BlockSpec((taps.shape[0], GROUP), lambda g: (0, g)),
            modal,
        ],
        out_specs=[pl.BlockSpec((rows, GROUP), lambda g: (0, g)), modal],
        out_shape=[
            jax.ShapeDtypeStruct((rows, width), BF16),
            jax.ShapeDtypeStruct(rates.shape, F32),
        ],
        scratch_shapes=[
            pltpu.VMEM((rows + SUBLANES, GROUP), F32),
            pltpu.VMEM((rows + SUBLANES, GROUP), F32),
            pltpu.VMEM((rows // SUBLANES, SUBLANES * SUBLANES, LANES), F32),
        ],
        compiler_params=vmem_params(32),
        cost_estimate=pl.CostEstimate(flops=rows * width, bytes_accessed=rows, transcendentals=0),
        name="mixed_and_states",
    )(streams, streams, halo, taps, rates)


def gated_rows(streams, halo, taps, mixed, skip, rates, residues, entering):
    rows, width = mixed.shape
    modes = rates.shape[0]
    modal = pl.BlockSpec((modes, SUBLANES, LANES), lambda g: (0, g, 0))
    return pl.pallas_call(
        gated_kernel,
        grid=(width // GROUP,),
        in_specs=[
            pl.BlockSpec((1, rows, GROUP), lambda g: (0, 0, g)),
            pl.BlockSpec((3, SUBLANES, GROUP), lambda g: (0, 0, g)),
            pl.BlockSpec((taps.shape[0], GROUP), lambda g: (0, g)),
            pl.BlockSpec((rows, GROUP), lambda g: (0, g)),
            pl.BlockSpec((1, GROUP), lambda g: (0, g)),
            modal,
            modal,
            modal,
        ],
        out_specs=pl.BlockSpec((rows, GROUP), lambda g: (0, g)),
        out_shape=jax.ShapeDtypeStruct((rows, width), BF16),
        scratch_shapes=[
            pltpu.VMEM((rows + SUBLANES, GROUP), F32),
            pltpu.VMEM((rows // SUBLANES, SUBLANES * SUBLANES, LANES), F32),
            pltpu.VMEM((rows // SUBLANES, SUBLANES * SUBLANES, LANES), F32),
        ],
        compiler_params=vmem_params(32),
        cost_estimate=pl.CostEstimate(flops=rows * width, bytes_accessed=rows, transcendentals=0),
        name="gated_rows",
    )(streams, halo, taps, mixed, skip, rates, residues, entering)


def entering_states(end, rates, rows, merges, before=None):
    place = lax.axis_index("seq")
    total, entering = end, jnp.zeros_like(end)
    held = []
    for bits in merges:
        span, count = 1 << bits[0], 1 << len(bits)
        if before and bits in before:
            total, *held = tied(total, *before[bits])
        others = [
            (mask, xor_permute(total, "seq", mask * span)) for mask in range(1, count)
        ]
        own = (place // span) % count
        inside = (place % span) * rows
        merged = jnp.zeros_like(total)
        for mask, value in [(0, total), *others]:
            run = own ^ mask
            gap = jnp.maximum(own - 1 - run, 0) * (span * rows) + inside
            ahead = jnp.exp(-rates * gap.astype(F32)) * value
            entering = entering + jnp.where(run < own, ahead, 0.0)
            gap = (count - 1 - run) * (span * rows)
            merged = merged + jnp.exp(-rates * gap.astype(F32)) * value
        total = merged
    return entering, held


def output_kernel(
    order_ref, added_ref, residual_ref, gain_ref, table_ref, block_ref, packed_ref, logits, squares
):
    at = pl.program_id(0)

    @pl.when(at == 0)
    def _():
        logits[...] = jnp.zeros_like(logits)
        squares[...] = jnp.zeros_like(squares)

    block = (residual_ref[...].astype(F32) + added_ref[0].astype(F32)).astype(BF16)
    block_ref[...] = block
    block_f = block.astype(F32)
    scaled = (block_f * gain_ref[...]).astype(BF16)
    logits[...] += lax.dot_general(
        table_ref[...], scaled, (((1,), (1,)), ((), ())), preferred_element_type=F32
    )
    squared = block_f * block_f
    width = squared.shape[1]
    for start in range(0, width, LANES):
        squares[...] += squared[:, start : start + LANES]

    @pl.when(at == pl.num_programs(0) - 1)
    def _():
        vocab = logits.shape[0]
        summed = jnp.sum(squares[...].T, axis=0, keepdims=True)
        high = summed.astype(BF16).astype(F32)
        row = lax.broadcasted_iota(jnp.int32, (16, summed.shape[1]), 0)
        extra = jnp.where(row == 0, high, jnp.where(row == 1, summed - high, 0.0))
        packed_ref[:vocab, :] = logits[...].astype(BF16)
        packed_ref[vocab:, :] = extra.astype(BF16)


def output_rows(order, added, residual_in, gain, table):
    parts, rows, width = added.shape
    vocab = table.shape[0]
    return pl.pallas_call(
        output_kernel,
        grid_spec=pltpu.PrefetchScalarGridSpec(
            num_scalar_prefetch=1,
            grid=(parts,),
            in_specs=[
                pl.BlockSpec((1, rows, width), lambda p, order: (order[p], 0, 0)),
                pl.BlockSpec((rows, width), lambda p, order: (0, p)),
                pl.BlockSpec((1, width), lambda p, order: (0, p)),
                pl.BlockSpec((vocab, width), lambda p, order: (0, p)),
            ],
            out_specs=[
                pl.BlockSpec((rows, width), lambda p, order: (0, p)),
                pl.BlockSpec((vocab + 16, rows), lambda p, order: (0, 0)),
            ],
            scratch_shapes=[
                pltpu.VMEM((vocab, rows), F32),
                pltpu.VMEM((rows, LANES), F32),
            ],
        ),
        out_shape=[
            jax.ShapeDtypeStruct(residual_in.shape, BF16),
            jax.ShapeDtypeStruct((vocab + 16, rows), BF16),
        ],
        compiler_params=vmem_params(32),
        cost_estimate=pl.CostEstimate(
            flops=2 * rows * parts * width * vocab,
            bytes_accessed=2 * parts * width * (3 * rows + vocab),
            transcendentals=0,
        ),
        name="output_rows",
    )(order, added, residual_in, gain, table)


def like_kernel(width, first_ref, second_ref, ids_ref, like_ref):
    rows = ids_ref.shape[1]
    vocab = first_ref.shape[0] - 16
    total = first_ref[...].astype(F32) + second_ref[...].astype(F32)
    squares = total[vocab : vocab + 1, :] + total[vocab + 1 : vocab + 2, :]
    inv_rms = lax.rsqrt(squares / width + 1e-06)
    logits = total[:vocab, :] * inv_rms
    largest = jnp.max(logits, axis=0, keepdims=True)
    summed = jnp.sum(jnp.exp(logits - largest), axis=0, keepdims=True)
    vocab_ids = lax.broadcasted_iota(jnp.int32, (vocab, rows), 0)
    chosen = jnp.sum(jnp.where(vocab_ids == ids_ref[...], logits, 0.0), axis=0, keepdims=True)
    like_ref[...] = chosen - (largest + jnp.log(summed))


def log_likelihood(first, second, next_ids, width):
    rows = next_ids.shape[0]
    like = pl.pallas_call(
        functools.partial(like_kernel, width),
        out_shape=jax.ShapeDtypeStruct((1, rows), F32),
        compiler_params=pltpu.CompilerParams(vmem_limit_bytes=16 * 1024 * 1024),
        name="log_likelihood",
    )(first, second, next_ids[None, :])
    return like[0]


def summed_over_chan(value):
    count = lax.axis_size("chan")
    total, span = value, 1
    while span < count // 2:
        total = (total.astype(F32) + xor_permute(total, "chan", span).astype(F32)).astype(BF16)
        span *= 2
    return total, xor_permute(total, "chan", span)


def tied(*values):
    return lax.optimization_barrier(values)


def column_pieces(weight, cuts):
    return [lax.slice_in_dim(weight, first, last, axis=1) for first, last in itertools.pairwise(cuts)]


def product(rows, weight):
    return jnp.dot(rows, weight, preferred_element_type=F32).astype(BF16)


def added_up(kept, other):
    return (kept.astype(F32) + other.astype(F32)).astype(BF16)


def placed_permute(value, same, seq_mask, chan_mask):
    count, chans = lax.axis_size("seq"), lax.axis_size("chan")
    pairs = []
    for place, chan in itertools.product(range(count), range(chans)):
        if (place // (count // chans) == chan) == same:
            target = (place ^ seq_mask) * chans + (chan ^ chan_mask)
            pairs.append((place * chans + chan, target))
    return lax.ppermute(value, ("seq", "chan"), pairs)


def projected_fast(gated, out_weight, core_weight, far):
    count, chans = lax.axis_size("seq"), lax.axis_size("chan")
    per_chan = count // chans
    rows, block = gated.shape[0], out_weight.shape[1]
    core, side, low, top = 1, 2, 4, per_chan
    here = lax.axis_index("seq") // per_chan == lax.axis_index("chan")
    part = rows // 2

    halves = [gated[:part], gated[part:]]
    above = [xor_permute(half, "seq", top) for half in halves]
    beside = xor_permute(gated, "seq", side)
    across = [xor_permute(above[0], "seq", side)]
    near = jnp.concatenate([out_weight, core_weight], axis=1)
    first = tied(jnp.concatenate([gated, beside], axis=0))[0]
    near_first = product(first, near)
    second = [tied(jnp.concatenate([above[0], across[0]], axis=0))[0]]
    near_second = [product(second[0], near)]
    above[1], far[1], _, _ = tied(above[1], far[1], near_first, near_second[0])
    across.append(xor_permute(above[1], "seq", side))
    far_all = jnp.concatenate(far + [xor_permute(piece, "seq", core) for piece in far], axis=1)
    second.append(tied(jnp.concatenate([above[1], across[1]], axis=0))[0])
    near_second.append(product(second[1], near))

    def first_sums(partial):
        total = added_up(partial, placed_permute(partial, False, 0, 1))
        return total[:rows], placed_permute(total[rows:], True, side, 0)

    def second_sums(close, distant):
        other = xor_permute(jnp.where(here, distant, close), "chan", 1)
        total = added_up(jnp.where(here, close, distant), other)
        back = [xor_permute(total[:part], "seq", top), xor_permute(total[part:], "seq", top | side)]
        hop = placed_permute(jnp.concatenate(back, axis=1), True, 0, 1)
        return back, jnp.split(hop, 2, axis=1)

    far_second = [product(rows_all, far_all) for rows_all in second]
    sums = [second_sums(*pair) for pair in zip(near_second, far_second)]
    near_sums = first_sums(near_first)
    far_sums = first_sums(product(first, far_all))
    blocks = {}
    for half, mask in itertools.product(range(2), (0, side)):
        span = slice(half * block, (half + 1) * block)
        at = mask // side
        for extra, own, moved in ((0, near_sums, 0), (low, far_sums, 1)):
            late = jnp.concatenate([pair[moved][at][:, span] for pair in sums], axis=0)
            blocks[mask | extra | (half * core)] = jnp.where(here, own[at][:, span], late)
    added = jnp.stack([blocks[mask] for mask in range(per_chan)])
    order = jnp.arange(per_chan, dtype=jnp.int32) ^ (lax.axis_index("seq") % per_chan)
    return added, order


def projected_plain(gated, out_weight):
    count, chans = lax.axis_size("seq"), lax.axis_size("chan")
    per_chan = count // chans
    partial = jnp.dot(
        gated,
        lax.all_gather(out_weight, "seq", axis=1, tiled=True),
        preferred_element_type=F32,
    )
    summed = lax.psum_scatter(partial, "chan", scatter_dimension=1, tiled=True)
    rows = gated.shape[0]
    added = summed.reshape(rows, per_chan, -1).transpose(1, 0, 2)
    return added, jnp.arange(per_chan, dtype=jnp.int32)


def local(
    features,
    residual_in,
    short_filter,
    decay_rates,
    residues,
    skip_gain,
    out_weight,
    final_gain,
    embedding,
    next_ids,
):
    rows, _, width = features.shape
    short_len = short_filter.shape[0]
    modes = decay_rates.shape[1]
    streams = jnp.transpose(features, (1, 0, 2))
    rim = shifted(features[rows - (short_len - 1) :], "seq", 1)
    halo = jnp.pad(
        jnp.transpose(rim, (1, 0, 2)).astype(F32), ((0, 0), (SUBLANES - (short_len - 1), 0), (0, 0))
    )
    taps = short_filter.reshape(short_len * 3, width)
    rates = decay_rates.T.reshape(modes, width // LANES, LANES)
    weights = residues.T.reshape(modes, width // LANES, LANES)
    count, chans = lax.axis_size("seq"), lax.axis_size("chan")
    fast = chans == 2 and count == 16
    top = count // chans
    if fast:
        block = out_weight.shape[1]
        low = top // 2
        far = column_pieces(out_weight, (0, block // 4, block))
        far[0] = xor_permute(far[0], "seq", low)
        core_weight = xor_permute(out_weight, "seq", 1)

    mixed, end = mixed_and_states(streams, halo, taps, rates)
    bits = range(count.bit_length() - 1)
    merges = [(bit,) for bit in bits]
    before = {(2,): far[:1]} if fast else None
    entering, held = entering_states(end, rates, rows, merges, before)
    if fast:
        entering, *waiting = tied(entering, *far[1:])
        far = held + [xor_permute(piece, "seq", low) for piece in waiting]
    if fast:
        entering, core_weight = tied(entering, core_weight)
    gated = gated_rows(streams, halo, taps, mixed, skip_gain[None, :], rates, weights, entering)
    if fast:
        added, order = projected_fast(gated, out_weight, core_weight, far)
    else:
        added, order = projected_plain(gated, out_weight)
    block_out, packed = output_rows(order, added, residual_in, final_gain[None, :], embedding)
    first, second = summed_over_chan(packed)
    return block_out, log_likelihood(first, second, next_ids, float(width * chans))


def solution(mesh):
    return jax.shard_map(
        local,
        mesh=mesh,
        in_specs=(
            P("seq", None, "chan"),
            P("seq", "chan"),
            P(None, None, "chan"),
            P("chan", None),
            P("chan", None),
            P("chan"),
            P("chan", "seq"),
            P("chan"),
            P(None, "chan"),
            P("seq"),
        ),
        out_specs=(P("seq", "chan"), P("seq")),
        check_vma=False,
    )
```

```python
import functools
import itertools

import jax
import jax.numpy as jnp
from jax import lax
from jax.experimental import pallas as pl
from jax.experimental.pallas import tpu as pltpu
from jax.sharding import PartitionSpec as P

F32 = jnp.float32
BF16 = jnp.bfloat16
LANES = 128
SUBLANES = 8
GROUP = LANES * SUBLANES


def xor_permute(value, axis, mask):
    count = lax.axis_size(axis)
    return lax.ppermute(value, axis, [(source, source ^ mask) for source in range(count)])


def shifted(value, axis, steps):
    count = lax.axis_size(axis)
    first, last = (max(0, -steps), min(count, count - steps))
    return lax.ppermute(value, axis, [(source, source + steps) for source in range(first, last)])


def fill_stream(scratch, halo, block):
    scratch[:SUBLANES, :] = halo
    scratch[SUBLANES:, :] = block.astype(F32)


def short_stream(scratch, taps_ref, stream, lanes, rows):
    taps = taps_ref.shape[0] // 3
    total = taps_ref[stream : stream + 1, lanes] * scratch[SUBLANES : SUBLANES + rows, lanes]
    for offset in range(1, taps):
        row = offset * 3 + stream
        start = SUBLANES - offset
        total = total + taps_ref[row : row + 1, lanes] * scratch[start : start + rows, lanes]
    return total


def lane_blocks():
    return [(part, slice(part * LANES, (part + 1) * LANES)) for part in range(SUBLANES)]


def states_kernel(
    keys_ref, values_ref, halo_ref, taps_ref, rates_ref, mixed_ref, end_ref, keys_f, values_f, rows_f
):
    rows = mixed_ref.shape[0]
    modes = rates_ref.shape[0]
    fill_stream(keys_f, halo_ref[1], keys_ref[0])
    fill_stream(values_f, halo_ref[2], values_ref[0])
    for part, lanes in lane_blocks():
        mixed = (
            short_stream(keys_f, taps_ref, 1, lanes, rows)
            * short_stream(values_f, taps_ref, 2, lanes, rows)
        ).astype(BF16)
        mixed_ref[:, lanes] = mixed
        rows_f[:, part * SUBLANES : (part + 1) * SUBLANES, :] = mixed.astype(F32).reshape(
            rows // SUBLANES, SUBLANES, LANES
        )
    decay = [jnp.exp(-rates_ref[mode]) for mode in range(modes)]

    def eight(block, states):
        for step in range(SUBLANES):
            entry = rows_f[block, pl.ds(step, SUBLANES, stride=SUBLANES), :]
            states = tuple(d * s + entry for d, s in zip(decay, states))
        return states

    zeros = tuple(jnp.zeros((SUBLANES, LANES), F32) for _ in range(modes))
    states = lax.fori_loop(0, rows // SUBLANES, eight, zeros)
    for mode in range(modes):
        end_ref[mode] = states[mode]


def gated_kernel(
    queries_ref,
    halo_ref,
    taps_ref,
    mixed_ref,
    skip_ref,
    rates_ref,
    residues_ref,
    enter_ref,
    gated_ref,
    queries_f,
    rows_f,
    long_f,
):
    rows = mixed_ref.shape[0]
    modes = rates_ref.shape[0]
    fill_stream(queries_f, halo_ref[0], queries_ref[0])
    for part, lanes in lane_blocks():
        rows_f[:, part * SUBLANES : (part + 1) * SUBLANES, :] = (
            mixed_ref[:, lanes].astype(F32).reshape(rows // SUBLANES, SUBLANES, LANES)
        )
    decay = [jnp.exp(-rates_ref[mode]) for mode in range(modes)]
    weight = [residues_ref[mode] for mode in range(modes)]

    def eight(block, states):
        for step in range(SUBLANES):
            entry = rows_f[block, pl.ds(step, SUBLANES, stride=SUBLANES), :]
            states = tuple(d * s + entry for d, s in zip(decay, states))
            terms = [w * s for w, s in zip(weight, states)]
            while len(terms) > 1:
                terms = [sum(terms[at : at + 2][1:], terms[at]) for at in range(0, len(terms), 2)]
            long_f[block, pl.ds(step, SUBLANES, stride=SUBLANES), :] = terms[0]
        return states

    lax.fori_loop(0, rows // SUBLANES, eight, tuple(enter_ref[mode] for mode in range(modes)))
    for part, lanes in lane_blocks():
        filtered = long_f[:, part * SUBLANES : (part + 1) * SUBLANES, :].reshape(rows, LANES)
        filtered = filtered.astype(BF16).astype(F32)
        direct = skip_ref[:, lanes] * mixed_ref[:, lanes].astype(F32)
        queries = short_stream(queries_f, taps_ref, 0, lanes, rows)
        gated_ref[:, lanes] = (queries * (filtered + direct)).astype(BF16)


def vmem_params(mib):
    return pltpu.CompilerParams(
        dimension_semantics=("arbitrary",), vmem_limit_bytes=mib * 1024 * 1024
    )


def mixed_and_states(streams, halo, taps, rates):
    rows, width = streams.shape[1:]
    modes = rates.shape[0]
    stream = lambda which: pl.BlockSpec((1, rows, GROUP), lambda g: (which, 0, g))
    modal = pl.BlockSpec((modes, SUBLANES, LANES), lambda g: (0, g, 0))
    return pl.pallas_call(
        states_kernel,
        grid=(width // GROUP,),
        in_specs=[
            stream(1),
            stream(2),
            pl.BlockSpec((3, SUBLANES, GROUP), lambda g: (0, 0, g)),
            pl.BlockSpec((taps.shape[0], GROUP), lambda g: (0, g)),
            modal,
        ],
        out_specs=[pl.BlockSpec((rows, GROUP), lambda g: (0, g)), modal],
        out_shape=[
            jax.ShapeDtypeStruct((rows, width), BF16),
            jax.ShapeDtypeStruct(rates.shape, F32),
        ],
        scratch_shapes=[
            pltpu.VMEM((rows + SUBLANES, GROUP), F32),
            pltpu.VMEM((rows + SUBLANES, GROUP), F32),
            pltpu.VMEM((rows // SUBLANES, SUBLANES * SUBLANES, LANES), F32),
        ],
        compiler_params=vmem_params(32),
        cost_estimate=pl.CostEstimate(flops=rows * width, bytes_accessed=rows, transcendentals=0),
        name="mixed_and_states",
    )(streams, streams, halo, taps, rates)


def gated_rows(streams, halo, taps, mixed, skip, rates, residues, entering):
    rows, width = mixed.shape
    modes = rates.shape[0]
    modal = pl.BlockSpec((modes, SUBLANES, LANES), lambda g: (0, g, 0))
    return pl.pallas_call(
        gated_kernel,
        grid=(width // GROUP,),
        in_specs=[
            pl.BlockSpec((1, rows, GROUP), lambda g: (0, 0, g)),
            pl.BlockSpec((3, SUBLANES, GROUP), lambda g: (0, 0, g)),
            pl.BlockSpec((taps.shape[0], GROUP), lambda g: (0, g)),
            pl.BlockSpec((rows, GROUP), lambda g: (0, g)),
            pl.BlockSpec((1, GROUP), lambda g: (0, g)),
            modal,
            modal,
            modal,
        ],
        out_specs=pl.BlockSpec((rows, GROUP), lambda g: (0, g)),
        out_shape=jax.ShapeDtypeStruct((rows, width), BF16),
        scratch_shapes=[
            pltpu.VMEM((rows + SUBLANES, GROUP), F32),
            pltpu.VMEM((rows // SUBLANES, SUBLANES * SUBLANES, LANES), F32),
            pltpu.VMEM((rows // SUBLANES, SUBLANES * SUBLANES, LANES), F32),
        ],
        compiler_params=vmem_params(32),
        cost_estimate=pl.CostEstimate(flops=rows * width, bytes_accessed=rows, transcendentals=0),
        name="gated_rows",
    )(streams, halo, taps, mixed, skip, rates, residues, entering)


def entering_states(end, rates, rows, merges, before=None, after=()):
    place = lax.axis_index("seq")
    total, entering = end, jnp.zeros_like(end)
    held = []
    for bits in merges:
        span, count = 1 << bits[0], 1 << len(bits)
        if before and bits in before:
            total, *held = tied(total, *before[bits])
        others = [
            (mask, xor_permute(total, "seq", mask * span)) for mask in range(1, count)
        ]
        if before and bits in before:
            value, *waiting = tied(others[0][1], *after)
            others = [(1, value)]
            held += waiting
        own = (place // span) % count
        inside = (place % span) * rows
        merged = jnp.zeros_like(total)
        for mask, value in [(0, total), *others]:
            run = own ^ mask
            gap = jnp.maximum(own - 1 - run, 0) * (span * rows) + inside
            ahead = jnp.exp(-rates * gap.astype(F32)) * value
            entering = entering + jnp.where(run < own, ahead, 0.0)
            gap = (count - 1 - run) * (span * rows)
            merged = merged + jnp.exp(-rates * gap.astype(F32)) * value
        total = merged
    return entering, held


def output_kernel(
    order_ref, added_ref, residual_ref, gain_ref, table_ref, block_ref, packed_ref, logits, squares
):
    at = pl.program_id(0)

    @pl.when(at == 0)
    def _():
        logits[...] = jnp.zeros_like(logits)
        squares[...] = jnp.zeros_like(squares)

    block = (residual_ref[...].astype(F32) + added_ref[0].astype(F32)).astype(BF16)
    block_ref[...] = block
    block_f = block.astype(F32)
    scaled = (block_f * gain_ref[...]).astype(BF16)
    logits[...] += lax.dot_general(
        table_ref[...], scaled, (((1,), (1,)), ((), ())), preferred_element_type=F32
    )
    squared = block_f * block_f
    width = squared.shape[1]
    for start in range(0, width, LANES):
        squares[...] += squared[:, start : start + LANES]

    @pl.when(at == pl.num_programs(0) - 1)
    def _():
        vocab = logits.shape[0]
        summed = jnp.sum(squares[...].T, axis=0, keepdims=True)
        high = summed.astype(BF16).astype(F32)
        row = lax.broadcasted_iota(jnp.int32, (16, summed.shape[1]), 0)
        extra = jnp.where(row == 0, high, jnp.where(row == 1, summed - high, 0.0))
        packed_ref[:vocab, :] = logits[...].astype(BF16)
        packed_ref[vocab:, :] = extra.astype(BF16)


def output_rows(order, added, residual_in, gain, table):
    parts, rows, width = added.shape
    vocab = table.shape[0]
    return pl.pallas_call(
        output_kernel,
        grid_spec=pltpu.PrefetchScalarGridSpec(
            num_scalar_prefetch=1,
            grid=(parts,),
            in_specs=[
                pl.BlockSpec((1, rows, width), lambda p, order: (order[p], 0, 0)),
                pl.BlockSpec((rows, width), lambda p, order: (0, p)),
                pl.BlockSpec((1, width), lambda p, order: (0, p)),
                pl.BlockSpec((vocab, width), lambda p, order: (0, p)),
            ],
            out_specs=[
                pl.BlockSpec((rows, width), lambda p, order: (0, p)),
                pl.BlockSpec((vocab + 16, rows), lambda p, order: (0, 0)),
            ],
            scratch_shapes=[
                pltpu.VMEM((vocab, rows), F32),
                pltpu.VMEM((rows, LANES), F32),
            ],
        ),
        out_shape=[
            jax.ShapeDtypeStruct(residual_in.shape, BF16),
            jax.ShapeDtypeStruct((vocab + 16, rows), BF16),
        ],
        compiler_params=vmem_params(32),
        cost_estimate=pl.CostEstimate(
            flops=2 * rows * parts * width * vocab,
            bytes_accessed=2 * parts * width * (3 * rows + vocab),
            transcendentals=0,
        ),
        name="output_rows",
    )(order, added, residual_in, gain, table)


def like_kernel(width, first_ref, second_ref, ids_ref, like_ref):
    rows = ids_ref.shape[1]
    vocab = first_ref.shape[0] - 16
    total = first_ref[...].astype(F32) + second_ref[...].astype(F32)
    squares = total[vocab : vocab + 1, :] + total[vocab + 1 : vocab + 2, :]
    inv_rms = lax.rsqrt(squares / width + 1e-06)
    logits = total[:vocab, :] * inv_rms
    largest = jnp.max(logits, axis=0, keepdims=True)
    summed = jnp.sum(jnp.exp(logits - largest), axis=0, keepdims=True)
    vocab_ids = lax.broadcasted_iota(jnp.int32, (vocab, rows), 0)
    chosen = jnp.sum(jnp.where(vocab_ids == ids_ref[...], logits, 0.0), axis=0, keepdims=True)
    like_ref[...] = chosen - (largest + jnp.log(summed))


def log_likelihood(first, second, next_ids, width):
    rows = next_ids.shape[0]
    like = pl.pallas_call(
        functools.partial(like_kernel, width),
        out_shape=jax.ShapeDtypeStruct((1, rows), F32),
        compiler_params=pltpu.CompilerParams(vmem_limit_bytes=16 * 1024 * 1024),
        name="log_likelihood",
    )(first, second, next_ids[None, :])
    return like[0]


def summed_over_chan(value):
    count = lax.axis_size("chan")
    total, span = value, 1
    while span < count // 2:
        total = (total.astype(F32) + xor_permute(total, "chan", span).astype(F32)).astype(BF16)
        span *= 2
    return total, xor_permute(total, "chan", span)


def tied(*values):
    return lax.optimization_barrier(values)


def column_pieces(weight, cuts):
    return [lax.slice_in_dim(weight, first, last, axis=1) for first, last in itertools.pairwise(cuts)]


def product(rows, weight):
    return jnp.dot(rows, weight, preferred_element_type=F32).astype(BF16)


def added_up(kept, other):
    return (kept.astype(F32) + other.astype(F32)).astype(BF16)


def placed_permute(value, same, seq_mask, chan_mask):
    count, chans = lax.axis_size("seq"), lax.axis_size("chan")
    pairs = []
    for place, chan in itertools.product(range(count), range(chans)):
        if (place // (count // chans) == chan) == same:
            target = (place ^ seq_mask) * chans + (chan ^ chan_mask)
            pairs.append((place * chans + chan, target))
    return lax.ppermute(value, ("seq", "chan"), pairs)


def projected_fast(gated, out_weight, core_weight, far):
    count, chans = lax.axis_size("seq"), lax.axis_size("chan")
    per_chan = count // chans
    rows, block = gated.shape[0], out_weight.shape[1]
    core, side, low, top = 1, 2, 4, per_chan
    here = lax.axis_index("seq") // per_chan == lax.axis_index("chan")
    part = rows // 2

    halves = [gated[:part], gated[part:]]
    above = [xor_permute(half, "seq", top) for half in halves]
    beside = xor_permute(gated, "seq", side)
    across = [xor_permute(above[0], "seq", side)]
    near = jnp.concatenate([out_weight, core_weight], axis=1)
    first = tied(jnp.concatenate([gated, beside], axis=0))[0]
    near_first = product(first, near)
    across[0], *far = tied(across[0], *far)
    second = [tied(jnp.concatenate([above[0], across[0]], axis=0))[0]]
    far_all = jnp.concatenate(far + [xor_permute(piece, "seq", core) for piece in far], axis=1)

    def first_sums(partial):
        total = added_up(partial, placed_permute(partial, False, 0, 1))
        return total[:rows], placed_permute(total[rows:], True, side, 0)

    def shared(rows_all):
        close, distant = product(rows_all, near), product(rows_all, far_all)
        return jnp.where(here, distant, close), jnp.where(here, close, distant)

    def second_sums(sent, kept):
        total = added_up(kept, xor_permute(sent, "chan", 1))
        back = [xor_permute(total[:part], "seq", top), xor_permute(total[part:], "seq", top | side)]
        hop = placed_permute(jnp.concatenate(back, axis=1), True, 0, 1)
        return back, jnp.split(hop, 2, axis=1)

    early = shared(second[0])
    above[1], *_ = tied(above[1], near_first, *early)
    across.append(xor_permute(above[1], "seq", side))
    second.append(tied(jnp.concatenate([above[1], across[1]], axis=0))[0])
    sums = [second_sums(*early), second_sums(*shared(second[1]))]
    near_sums = first_sums(near_first)
    far_sums = first_sums(product(first, far_all))
    blocks = {}
    for half, mask in itertools.product(range(2), (0, side)):
        span = slice(half * block, (half + 1) * block)
        at = mask // side
        for extra, own, moved in ((0, near_sums, 0), (low, far_sums, 1)):
            late = jnp.concatenate([pair[moved][at][:, span] for pair in sums], axis=0)
            blocks[mask | extra | (half * core)] = jnp.where(here, own[at][:, span], late)
    added = jnp.stack([blocks[mask] for mask in range(per_chan)])
    order = jnp.arange(per_chan, dtype=jnp.int32) ^ (lax.axis_index("seq") % per_chan)
    return added, order


def projected_plain(gated, out_weight):
    count, chans = lax.axis_size("seq"), lax.axis_size("chan")
    per_chan = count // chans
    partial = jnp.dot(
        gated,
        lax.all_gather(out_weight, "seq", axis=1, tiled=True),
        preferred_element_type=F32,
    )
    summed = lax.psum_scatter(partial, "chan", scatter_dimension=1, tiled=True)
    rows = gated.shape[0]
    added = summed.reshape(rows, per_chan, -1).transpose(1, 0, 2)
    return added, jnp.arange(per_chan, dtype=jnp.int32)


def local(
    features,
    residual_in,
    short_filter,
    decay_rates,
    residues,
    skip_gain,
    out_weight,
    final_gain,
    embedding,
    next_ids,
):
    rows, _, width = features.shape
    short_len = short_filter.shape[0]
    modes = decay_rates.shape[1]
    streams = jnp.transpose(features, (1, 0, 2))
    rim = shifted(features[rows - (short_len - 1) :], "seq", 1)
    halo = jnp.pad(
        jnp.transpose(rim, (1, 0, 2)).astype(F32), ((0, 0), (SUBLANES - (short_len - 1), 0), (0, 0))
    )
    taps = short_filter.reshape(short_len * 3, width)
    rates = decay_rates.T.reshape(modes, width // LANES, LANES)
    weights = residues.T.reshape(modes, width // LANES, LANES)
    count, chans = lax.axis_size("seq"), lax.axis_size("chan")
    fast = chans == 2 and count == 16
    top = count // chans
    if fast:
        block = out_weight.shape[1]
        low = top // 2
        far = column_pieces(out_weight, (0, block // 4, block))
        far[0] = xor_permute(far[0], "seq", low)
        core_weight = xor_permute(out_weight, "seq", 1)

    mixed, end = mixed_and_states(streams, halo, taps, rates)
    bits = range(count.bit_length() - 1)
    merges = [(bit,) for bit in bits]
    before = {(2,): far[:1]} if fast else None
    after = far[1:] if fast else ()
    entering, held = entering_states(end, rates, rows, merges, before, after)
    if fast:
        far = held[:1] + [xor_permute(held[1], "seq", low)]
    if fast:
        entering, core_weight = tied(entering, core_weight)
    gated = gated_rows(streams, halo, taps, mixed, skip_gain[None, :], rates, weights, entering)
    if fast:
        added, order = projected_fast(gated, out_weight, core_weight, far)
    else:
        added, order = projected_plain(gated, out_weight)
    block_out, packed = output_rows(order, added, residual_in, final_gain[None, :], embedding)
    first, second = summed_over_chan(packed)
    return block_out, log_likelihood(first, second, next_ids, float(width * chans))


def solution(mesh):
    return jax.shard_map(
        local,
        mesh=mesh,
        in_specs=(
            P("seq", None, "chan"),
            P("seq", "chan"),
            P(None, None, "chan"),
            P("chan", None),
            P("chan", None),
            P("chan"),
            P("chan", "seq"),
            P("chan"),
            P(None, "chan"),
            P("seq"),
        ),
        out_specs=(P("seq", "chan"), P("seq")),
        check_vma=False,
    )
```

```python
import functools
import itertools

import jax
import jax.numpy as jnp
from jax import lax
from jax.experimental import pallas as pl
from jax.experimental.pallas import tpu as pltpu
from jax.sharding import PartitionSpec as P

F32 = jnp.float32
BF16 = jnp.bfloat16
LANES = 128
SUBLANES = 8
GROUP = LANES * SUBLANES


def xor_permute(value, axis, mask):
    count = lax.axis_size(axis)
    return lax.ppermute(value, axis, [(source, source ^ mask) for source in range(count)])


def shifted(value, axis, steps):
    count = lax.axis_size(axis)
    first, last = (max(0, -steps), min(count, count - steps))
    return lax.ppermute(value, axis, [(source, source + steps) for source in range(first, last)])


def fill_stream(scratch, halo, block):
    scratch[:SUBLANES, :] = halo
    scratch[SUBLANES:, :] = block.astype(F32)


def short_stream(scratch, taps_ref, stream, lanes, rows):
    taps = taps_ref.shape[0] // 3
    total = taps_ref[stream : stream + 1, lanes] * scratch[SUBLANES : SUBLANES + rows, lanes]
    for offset in range(1, taps):
        row = offset * 3 + stream
        start = SUBLANES - offset
        total = total + taps_ref[row : row + 1, lanes] * scratch[start : start + rows, lanes]
    return total


def lane_blocks():
    return [(part, slice(part * LANES, (part + 1) * LANES)) for part in range(SUBLANES)]


def states_kernel(
    keys_ref, values_ref, halo_ref, taps_ref, rates_ref, mixed_ref, end_ref, keys_f, values_f, rows_f
):
    rows = mixed_ref.shape[0]
    modes = rates_ref.shape[0]
    fill_stream(keys_f, halo_ref[1], keys_ref[0])
    fill_stream(values_f, halo_ref[2], values_ref[0])
    for part, lanes in lane_blocks():
        mixed = (
            short_stream(keys_f, taps_ref, 1, lanes, rows)
            * short_stream(values_f, taps_ref, 2, lanes, rows)
        ).astype(BF16)
        mixed_ref[:, lanes] = mixed
        rows_f[:, part * SUBLANES : (part + 1) * SUBLANES, :] = mixed.astype(F32).reshape(
            rows // SUBLANES, SUBLANES, LANES
        )
    decay = [jnp.exp(-rates_ref[mode]) for mode in range(modes)]

    def eight(block, states):
        for step in range(SUBLANES):
            entry = rows_f[block, pl.ds(step, SUBLANES, stride=SUBLANES), :]
            states = tuple(d * s + entry for d, s in zip(decay, states))
        return states

    zeros = tuple(jnp.zeros((SUBLANES, LANES), F32) for _ in range(modes))
    states = lax.fori_loop(0, rows // SUBLANES, eight, zeros)
    for mode in range(modes):
        end_ref[mode] = states[mode]


def gated_kernel(
    queries_ref,
    halo_ref,
    taps_ref,
    mixed_ref,
    skip_ref,
    rates_ref,
    residues_ref,
    enter_ref,
    gated_ref,
    queries_f,
    rows_f,
    long_f,
):
    rows = mixed_ref.shape[0]
    modes = rates_ref.shape[0]
    fill_stream(queries_f, halo_ref[0], queries_ref[0])
    for part, lanes in lane_blocks():
        rows_f[:, part * SUBLANES : (part + 1) * SUBLANES, :] = (
            mixed_ref[:, lanes].astype(F32).reshape(rows // SUBLANES, SUBLANES, LANES)
        )
    decay = [jnp.exp(-rates_ref[mode]) for mode in range(modes)]
    weight = [residues_ref[mode] for mode in range(modes)]

    def eight(block, states):
        for step in range(SUBLANES):
            entry = rows_f[block, pl.ds(step, SUBLANES, stride=SUBLANES), :]
            states = tuple(d * s + entry for d, s in zip(decay, states))
            terms = [w * s for w, s in zip(weight, states)]
            while len(terms) > 1:
                terms = [sum(terms[at : at + 2][1:], terms[at]) for at in range(0, len(terms), 2)]
            long_f[block, pl.ds(step, SUBLANES, stride=SUBLANES), :] = terms[0]
        return states

    lax.fori_loop(0, rows // SUBLANES, eight, tuple(enter_ref[mode] for mode in range(modes)))
    for part, lanes in lane_blocks():
        filtered = long_f[:, part * SUBLANES : (part + 1) * SUBLANES, :].reshape(rows, LANES)
        filtered = filtered.astype(BF16).astype(F32)
        direct = skip_ref[:, lanes] * mixed_ref[:, lanes].astype(F32)
        queries = short_stream(queries_f, taps_ref, 0, lanes, rows)
        gated_ref[:, lanes] = (queries * (filtered + direct)).astype(BF16)


def vmem_params(mib):
    return pltpu.CompilerParams(
        dimension_semantics=("arbitrary",), vmem_limit_bytes=mib * 1024 * 1024
    )


def mixed_and_states(streams, halo, taps, rates):
    rows, width = streams.shape[1:]
    modes = rates.shape[0]
    stream = lambda which: pl.BlockSpec((1, rows, GROUP), lambda g: (which, 0, g))
    modal = pl.BlockSpec((modes, SUBLANES, LANES), lambda g: (0, g, 0))
    return pl.pallas_call(
        states_kernel,
        grid=(width // GROUP,),
        in_specs=[
            stream(1),
            stream(2),
            pl.BlockSpec((3, SUBLANES, GROUP), lambda g: (0, 0, g)),
            pl.BlockSpec((taps.shape[0], GROUP), lambda g: (0, g)),
            modal,
        ],
        out_specs=[pl.BlockSpec((rows, GROUP), lambda g: (0, g)), modal],
        out_shape=[
            jax.ShapeDtypeStruct((rows, width), BF16),
            jax.ShapeDtypeStruct(rates.shape, F32),
        ],
        scratch_shapes=[
            pltpu.VMEM((rows + SUBLANES, GROUP), F32),
            pltpu.VMEM((rows + SUBLANES, GROUP), F32),
            pltpu.VMEM((rows // SUBLANES, SUBLANES * SUBLANES, LANES), F32),
        ],
        compiler_params=vmem_params(32),
        cost_estimate=pl.CostEstimate(flops=rows * width, bytes_accessed=rows, transcendentals=0),
        name="mixed_and_states",
    )(streams, streams, halo, taps, rates)


def gated_rows(streams, halo, taps, mixed, skip, rates, residues, entering):
    rows, width = mixed.shape
    modes = rates.shape[0]
    modal = pl.BlockSpec((modes, SUBLANES, LANES), lambda g: (0, g, 0))
    return pl.pallas_call(
        gated_kernel,
        grid=(width // GROUP,),
        in_specs=[
            pl.BlockSpec((1, rows, GROUP), lambda g: (0, 0, g)),
            pl.BlockSpec((3, SUBLANES, GROUP), lambda g: (0, 0, g)),
            pl.BlockSpec((taps.shape[0], GROUP), lambda g: (0, g)),
            pl.BlockSpec((rows, GROUP), lambda g: (0, g)),
            pl.BlockSpec((1, GROUP), lambda g: (0, g)),
            modal,
            modal,
            modal,
        ],
        out_specs=pl.BlockSpec((rows, GROUP), lambda g: (0, g)),
        out_shape=jax.ShapeDtypeStruct((rows, width), BF16),
        scratch_shapes=[
            pltpu.VMEM((rows + SUBLANES, GROUP), F32),
            pltpu.VMEM((rows // SUBLANES, SUBLANES * SUBLANES, LANES), F32),
            pltpu.VMEM((rows // SUBLANES, SUBLANES * SUBLANES, LANES), F32),
        ],
        compiler_params=vmem_params(32),
        cost_estimate=pl.CostEstimate(flops=rows * width, bytes_accessed=rows, transcendentals=0),
        name="gated_rows",
    )(streams, halo, taps, mixed, skip, rates, residues, entering)


def entering_states(end, rates, rows, merges, before=None, after=()):
    place = lax.axis_index("seq")
    total, entering = end, jnp.zeros_like(end)
    held = []
    for bits in merges:
        span, count = 1 << bits[0], 1 << len(bits)
        if before and bits in before:
            total, *held = tied(total, *before[bits])
        others = [
            (mask, xor_permute(total, "seq", mask * span)) for mask in range(1, count)
        ]
        if before and bits in before:
            value, *waiting = tied(others[0][1], *after)
            others = [(1, value)]
            held += waiting
        own = (place // span) % count
        inside = (place % span) * rows
        merged = jnp.zeros_like(total)
        for mask, value in [(0, total), *others]:
            run = own ^ mask
            gap = jnp.maximum(own - 1 - run, 0) * (span * rows) + inside
            ahead = jnp.exp(-rates * gap.astype(F32)) * value
            entering = entering + jnp.where(run < own, ahead, 0.0)
            gap = (count - 1 - run) * (span * rows)
            merged = merged + jnp.exp(-rates * gap.astype(F32)) * value
        total = merged
    return entering, held


def output_kernel(
    order_ref, added_ref, residual_ref, gain_ref, table_ref, block_ref, packed_ref, logits, squares
):
    at = pl.program_id(0)

    @pl.when(at == 0)
    def _():
        logits[...] = jnp.zeros_like(logits)
        squares[...] = jnp.zeros_like(squares)

    block = (residual_ref[...].astype(F32) + added_ref[0].astype(F32)).astype(BF16)
    block_ref[...] = block
    block_f = block.astype(F32)
    scaled = (block_f * gain_ref[...]).astype(BF16)
    logits[...] += lax.dot_general(
        table_ref[...], scaled, (((1,), (1,)), ((), ())), preferred_element_type=F32
    )
    squared = block_f * block_f
    width = squared.shape[1]
    for start in range(0, width, LANES):
        squares[...] += squared[:, start : start + LANES]

    @pl.when(at == pl.num_programs(0) - 1)
    def _():
        vocab = logits.shape[0]
        summed = jnp.sum(squares[...].T, axis=0, keepdims=True)
        high = summed.astype(BF16).astype(F32)
        row = lax.broadcasted_iota(jnp.int32, (16, summed.shape[1]), 0)
        extra = jnp.where(row == 0, high, jnp.where(row == 1, summed - high, 0.0))
        packed_ref[:vocab, :] = logits[...].astype(BF16)
        packed_ref[vocab:, :] = extra.astype(BF16)


def output_rows(order, added, residual_in, gain, table):
    parts, rows, width = added.shape
    vocab = table.shape[0]
    return pl.pallas_call(
        output_kernel,
        grid_spec=pltpu.PrefetchScalarGridSpec(
            num_scalar_prefetch=1,
            grid=(parts,),
            in_specs=[
                pl.BlockSpec((1, rows, width), lambda p, order: (order[p], 0, 0)),
                pl.BlockSpec((rows, width), lambda p, order: (0, p)),
                pl.BlockSpec((1, width), lambda p, order: (0, p)),
                pl.BlockSpec((vocab, width), lambda p, order: (0, p)),
            ],
            out_specs=[
                pl.BlockSpec((rows, width), lambda p, order: (0, p)),
                pl.BlockSpec((vocab + 16, rows), lambda p, order: (0, 0)),
            ],
            scratch_shapes=[
                pltpu.VMEM((vocab, rows), F32),
                pltpu.VMEM((rows, LANES), F32),
            ],
        ),
        out_shape=[
            jax.ShapeDtypeStruct(residual_in.shape, BF16),
            jax.ShapeDtypeStruct((vocab + 16, rows), BF16),
        ],
        compiler_params=vmem_params(32),
        cost_estimate=pl.CostEstimate(
            flops=2 * rows * parts * width * vocab,
            bytes_accessed=2 * parts * width * (3 * rows + vocab),
            transcendentals=0,
        ),
        name="output_rows",
    )(order, added, residual_in, gain, table)


def like_kernel(width, first_ref, second_ref, ids_ref, like_ref):
    rows = ids_ref.shape[1]
    vocab = first_ref.shape[0] - 16
    total = first_ref[...].astype(F32) + second_ref[...].astype(F32)
    squares = total[vocab : vocab + 1, :] + total[vocab + 1 : vocab + 2, :]
    inv_rms = lax.rsqrt(squares / width + 1e-06)
    logits = total[:vocab, :] * inv_rms
    largest = jnp.max(logits, axis=0, keepdims=True)
    summed = jnp.sum(jnp.exp(logits - largest), axis=0, keepdims=True)
    vocab_ids = lax.broadcasted_iota(jnp.int32, (vocab, rows), 0)
    chosen = jnp.sum(jnp.where(vocab_ids == ids_ref[...], logits, 0.0), axis=0, keepdims=True)
    like_ref[...] = chosen - (largest + jnp.log(summed))


def log_likelihood(first, second, next_ids, width):
    rows = next_ids.shape[0]
    like = pl.pallas_call(
        functools.partial(like_kernel, width),
        out_shape=jax.ShapeDtypeStruct((1, rows), F32),
        compiler_params=pltpu.CompilerParams(vmem_limit_bytes=16 * 1024 * 1024),
        name="log_likelihood",
    )(first, second, next_ids[None, :])
    return like[0]


def summed_over_chan(value):
    count = lax.axis_size("chan")
    total, span = value, 1
    while span < count // 2:
        total = (total.astype(F32) + xor_permute(total, "chan", span).astype(F32)).astype(BF16)
        span *= 2
    return total, xor_permute(total, "chan", span)


def tied(*values):
    return lax.optimization_barrier(values)


def column_pieces(weight, cuts):
    return [lax.slice_in_dim(weight, first, last, axis=1) for first, last in itertools.pairwise(cuts)]


def product(rows, weight):
    return jnp.dot(rows, weight, preferred_element_type=F32).astype(BF16)


def added_up(kept, other):
    return (kept.astype(F32) + other.astype(F32)).astype(BF16)


def placed_permute(value, same, seq_mask, chan_mask):
    count, chans = lax.axis_size("seq"), lax.axis_size("chan")
    pairs = []
    for place, chan in itertools.product(range(count), range(chans)):
        if (place // (count // chans) == chan) == same:
            target = (place ^ seq_mask) * chans + (chan ^ chan_mask)
            pairs.append((place * chans + chan, target))
    return lax.ppermute(value, ("seq", "chan"), pairs)


def projected_fast(gated, out_weight, core_weight, far):
    count, chans = lax.axis_size("seq"), lax.axis_size("chan")
    per_chan = count // chans
    rows, block = gated.shape[0], out_weight.shape[1]
    core, side, low, top = 1, 2, 4, per_chan
    here = lax.axis_index("seq") // per_chan == lax.axis_index("chan")
    part = rows // 2

    halves = [gated[:part], gated[part:]]
    above = [xor_permute(half, "seq", top) for half in halves]
    beside = xor_permute(gated, "seq", side)
    across = [xor_permute(above[0], "seq", side)]
    near = jnp.concatenate([out_weight, core_weight], axis=1)
    first = tied(jnp.concatenate([gated, beside], axis=0))[0]
    near_first = product(first, near)
    across[0], *far = tied(across[0], *far)
    second = [tied(jnp.concatenate([above[0], across[0]], axis=0))[0]]
    far_all = jnp.concatenate(far + [xor_permute(piece, "seq", core) for piece in far], axis=1)

    def first_sums(partial, *after):
        other, *_ = tied(placed_permute(partial, False, 0, 1), *after)
        total = added_up(partial, other)
        return total[:rows], placed_permute(total[rows:], True, side, 0)

    def shared(rows_all):
        close, distant = product(rows_all, near), product(rows_all, far_all)
        return jnp.where(here, distant, close), jnp.where(here, close, distant)

    def second_sums(sent, kept, *after):
        other, *_ = tied(xor_permute(sent, "chan", 1), *after)
        total = added_up(kept, other)
        back = [xor_permute(total[:part], "seq", top), xor_permute(total[part:], "seq", top | side)]
        hop = placed_permute(jnp.concatenate(back, axis=1), True, 0, 1)
        return back, jnp.split(hop, 2, axis=1)

    early = shared(second[0])
    above[1], *_ = tied(above[1], near_first, *early)
    across.append(xor_permute(above[1], "seq", side))
    second.append(tied(jnp.concatenate([above[1], across[1]], axis=0))[0])
    late = shared(second[1])
    sums = [second_sums(*early, across[1]), second_sums(*late)]
    near_sums = first_sums(near_first, across[1])
    far_first, _ = tied(product(first, far_all), late[0])
    far_sums = first_sums(far_first)
    blocks = {}
    for half, mask in itertools.product(range(2), (0, side)):
        span = slice(half * block, (half + 1) * block)
        at = mask // side
        for extra, own, moved in ((0, near_sums, 0), (low, far_sums, 1)):
            late = jnp.concatenate([pair[moved][at][:, span] for pair in sums], axis=0)
            blocks[mask | extra | (half * core)] = jnp.where(here, own[at][:, span], late)
    added = jnp.stack([blocks[mask] for mask in range(per_chan)])
    order = jnp.arange(per_chan, dtype=jnp.int32) ^ (lax.axis_index("seq") % per_chan)
    return added, order


def projected_plain(gated, out_weight):
    count, chans = lax.axis_size("seq"), lax.axis_size("chan")
    per_chan = count // chans
    partial = jnp.dot(
        gated,
        lax.all_gather(out_weight, "seq", axis=1, tiled=True),
        preferred_element_type=F32,
    )
    summed = lax.psum_scatter(partial, "chan", scatter_dimension=1, tiled=True)
    rows = gated.shape[0]
    added = summed.reshape(rows, per_chan, -1).transpose(1, 0, 2)
    return added, jnp.arange(per_chan, dtype=jnp.int32)


def local(
    features,
    residual_in,
    short_filter,
    decay_rates,
    residues,
    skip_gain,
    out_weight,
    final_gain,
    embedding,
    next_ids,
):
    rows, _, width = features.shape
    short_len = short_filter.shape[0]
    modes = decay_rates.shape[1]
    streams = jnp.transpose(features, (1, 0, 2))
    rim = shifted(features[rows - (short_len - 1) :], "seq", 1)
    halo = jnp.pad(
        jnp.transpose(rim, (1, 0, 2)).astype(F32), ((0, 0), (SUBLANES - (short_len - 1), 0), (0, 0))
    )
    taps = short_filter.reshape(short_len * 3, width)
    rates = decay_rates.T.reshape(modes, width // LANES, LANES)
    weights = residues.T.reshape(modes, width // LANES, LANES)
    count, chans = lax.axis_size("seq"), lax.axis_size("chan")
    fast = chans == 2 and count == 16
    top = count // chans
    if fast:
        block = out_weight.shape[1]
        low = top // 2
        far = column_pieces(out_weight, (0, block // 4, block))
        far[0] = xor_permute(far[0], "seq", low)
        core_weight = xor_permute(out_weight, "seq", 1)

    mixed, end = mixed_and_states(streams, halo, taps, rates)
    bits = range(count.bit_length() - 1)
    merges = [(bit,) for bit in bits]
    before = {(2,): far[:1]} if fast else None
    after = far[1:] if fast else ()
    entering, held = entering_states(end, rates, rows, merges, before, after)
    if fast:
        far = held[:1] + [xor_permute(held[1], "seq", low)]
    if fast:
        entering, core_weight = tied(entering, core_weight)
    gated = gated_rows(streams, halo, taps, mixed, skip_gain[None, :], rates, weights, entering)
    if fast:
        added, order = projected_fast(gated, out_weight, core_weight, far)
    else:
        added, order = projected_plain(gated, out_weight)
    block_out, packed = output_rows(order, added, residual_in, final_gain[None, :], embedding)
    first, second = summed_over_chan(packed)
    return block_out, log_likelihood(first, second, next_ids, float(width * chans))


def solution(mesh):
    return jax.shard_map(
        local,
        mesh=mesh,
        in_specs=(
            P("seq", None, "chan"),
            P("seq", "chan"),
            P(None, None, "chan"),
            P("chan", None),
            P("chan", None),
            P("chan"),
            P("chan", "seq"),
            P("chan"),
            P(None, "chan"),
            P("seq"),
        ),
        out_specs=(P("seq", "chan"), P("seq")),
        check_vma=False,
    )
```

```python
import functools
import itertools

import jax
import jax.numpy as jnp
from jax import lax
from jax.experimental import pallas as pl
from jax.experimental.pallas import tpu as pltpu
from jax.sharding import PartitionSpec as P

F32 = jnp.float32
BF16 = jnp.bfloat16
LANES = 128
SUBLANES = 8
GROUP = LANES * SUBLANES


def xor_permute(value, axis, mask):
    count = lax.axis_size(axis)
    return lax.ppermute(value, axis, [(source, source ^ mask) for source in range(count)])


def shifted(value, axis, steps):
    count = lax.axis_size(axis)
    first, last = (max(0, -steps), min(count, count - steps))
    return lax.ppermute(value, axis, [(source, source + steps) for source in range(first, last)])


def fill_stream(scratch, halo, block):
    scratch[:SUBLANES, :] = halo
    scratch[SUBLANES:, :] = block.astype(F32)


def short_stream(scratch, taps_ref, stream, lanes, rows):
    taps = taps_ref.shape[0] // 3
    total = taps_ref[stream : stream + 1, lanes] * scratch[SUBLANES : SUBLANES + rows, lanes]
    for offset in range(1, taps):
        row = offset * 3 + stream
        start = SUBLANES - offset
        total = total + taps_ref[row : row + 1, lanes] * scratch[start : start + rows, lanes]
    return total


def lane_blocks():
    return [(part, slice(part * LANES, (part + 1) * LANES)) for part in range(SUBLANES)]


def states_kernel(
    keys_ref, values_ref, halo_ref, taps_ref, rates_ref, mixed_ref, end_ref, keys_f, values_f, rows_f
):
    rows = mixed_ref.shape[0]
    modes = rates_ref.shape[0]
    fill_stream(keys_f, halo_ref[1], keys_ref[0])
    fill_stream(values_f, halo_ref[2], values_ref[0])
    for part, lanes in lane_blocks():
        mixed = (
            short_stream(keys_f, taps_ref, 1, lanes, rows)
            * short_stream(values_f, taps_ref, 2, lanes, rows)
        ).astype(BF16)
        mixed_ref[:, lanes] = mixed
        rows_f[:, part * SUBLANES : (part + 1) * SUBLANES, :] = mixed.astype(F32).reshape(
            rows // SUBLANES, SUBLANES, LANES
        )
    decay = [jnp.exp(-rates_ref[mode]) for mode in range(modes)]

    def eight(block, states):
        for step in range(SUBLANES):
            entry = rows_f[block, pl.ds(step, SUBLANES, stride=SUBLANES), :]
            states = tuple(d * s + entry for d, s in zip(decay, states))
        return states

    zeros = tuple(jnp.zeros((SUBLANES, LANES), F32) for _ in range(modes))
    states = lax.fori_loop(0, rows // SUBLANES, eight, zeros)
    for mode in range(modes):
        end_ref[mode] = states[mode]


def gated_kernel(
    queries_ref,
    halo_ref,
    taps_ref,
    mixed_ref,
    skip_ref,
    rates_ref,
    residues_ref,
    enter_ref,
    gated_ref,
    queries_f,
    rows_f,
    long_f,
):
    rows = mixed_ref.shape[0]
    modes = rates_ref.shape[0]
    fill_stream(queries_f, halo_ref[0], queries_ref[0])
    for part, lanes in lane_blocks():
        rows_f[:, part * SUBLANES : (part + 1) * SUBLANES, :] = (
            mixed_ref[:, lanes].astype(F32).reshape(rows // SUBLANES, SUBLANES, LANES)
        )
    decay = [jnp.exp(-rates_ref[mode]) for mode in range(modes)]
    weight = [residues_ref[mode] for mode in range(modes)]

    def eight(block, states):
        for step in range(SUBLANES):
            entry = rows_f[block, pl.ds(step, SUBLANES, stride=SUBLANES), :]
            states = tuple(d * s + entry for d, s in zip(decay, states))
            terms = [w * s for w, s in zip(weight, states)]
            while len(terms) > 1:
                terms = [sum(terms[at : at + 2][1:], terms[at]) for at in range(0, len(terms), 2)]
            long_f[block, pl.ds(step, SUBLANES, stride=SUBLANES), :] = terms[0]
        return states

    lax.fori_loop(0, rows // SUBLANES, eight, tuple(enter_ref[mode] for mode in range(modes)))
    for part, lanes in lane_blocks():
        filtered = long_f[:, part * SUBLANES : (part + 1) * SUBLANES, :].reshape(rows, LANES)
        filtered = filtered.astype(BF16).astype(F32)
        direct = skip_ref[:, lanes] * mixed_ref[:, lanes].astype(F32)
        queries = short_stream(queries_f, taps_ref, 0, lanes, rows)
        gated_ref[:, lanes] = (queries * (filtered + direct)).astype(BF16)


def vmem_params(mib):
    return pltpu.CompilerParams(
        dimension_semantics=("arbitrary",), vmem_limit_bytes=mib * 1024 * 1024
    )


def mixed_and_states(streams, halo, taps, rates):
    rows, width = streams.shape[1:]
    modes = rates.shape[0]
    stream = lambda which: pl.BlockSpec((1, rows, GROUP), lambda g: (which, 0, g))
    modal = pl.BlockSpec((modes, SUBLANES, LANES), lambda g: (0, g, 0))
    return pl.pallas_call(
        states_kernel,
        grid=(width // GROUP,),
        in_specs=[
            stream(1),
            stream(2),
            pl.BlockSpec((3, SUBLANES, GROUP), lambda g: (0, 0, g)),
            pl.BlockSpec((taps.shape[0], GROUP), lambda g: (0, g)),
            modal,
        ],
        out_specs=[pl.BlockSpec((rows, GROUP), lambda g: (0, g)), modal],
        out_shape=[
            jax.ShapeDtypeStruct((rows, width), BF16),
            jax.ShapeDtypeStruct(rates.shape, F32),
        ],
        scratch_shapes=[
            pltpu.VMEM((rows + SUBLANES, GROUP), F32),
            pltpu.VMEM((rows + SUBLANES, GROUP), F32),
            pltpu.VMEM((rows // SUBLANES, SUBLANES * SUBLANES, LANES), F32),
        ],
        compiler_params=vmem_params(32),
        cost_estimate=pl.CostEstimate(flops=rows * width, bytes_accessed=rows, transcendentals=0),
        name="mixed_and_states",
    )(streams, streams, halo, taps, rates)


def gated_rows(streams, halo, taps, mixed, skip, rates, residues, entering):
    rows, width = mixed.shape
    modes = rates.shape[0]
    modal = pl.BlockSpec((modes, SUBLANES, LANES), lambda g: (0, g, 0))
    return pl.pallas_call(
        gated_kernel,
        grid=(width // GROUP,),
        in_specs=[
            pl.BlockSpec((1, rows, GROUP), lambda g: (0, 0, g)),
            pl.BlockSpec((3, SUBLANES, GROUP), lambda g: (0, 0, g)),
            pl.BlockSpec((taps.shape[0], GROUP), lambda g: (0, g)),
            pl.BlockSpec((rows, GROUP), lambda g: (0, g)),
            pl.BlockSpec((1, GROUP), lambda g: (0, g)),
            modal,
            modal,
            modal,
        ],
        out_specs=pl.BlockSpec((rows, GROUP), lambda g: (0, g)),
        out_shape=jax.ShapeDtypeStruct((rows, width), BF16),
        scratch_shapes=[
            pltpu.VMEM((rows + SUBLANES, GROUP), F32),
            pltpu.VMEM((rows // SUBLANES, SUBLANES * SUBLANES, LANES), F32),
            pltpu.VMEM((rows // SUBLANES, SUBLANES * SUBLANES, LANES), F32),
        ],
        compiler_params=vmem_params(32),
        cost_estimate=pl.CostEstimate(flops=rows * width, bytes_accessed=rows, transcendentals=0),
        name="gated_rows",
    )(streams, halo, taps, mixed, skip, rates, residues, entering)


def entering_states(end, rates, rows, merges, before=None, after=()):
    place = lax.axis_index("seq")
    total, entering = end, jnp.zeros_like(end)
    held = []
    for bits in merges:
        span, count = 1 << bits[0], 1 << len(bits)
        if before and bits in before:
            total, *held = tied(total, *before[bits])
        others = [
            (mask, xor_permute(total, "seq", mask * span)) for mask in range(1, count)
        ]
        if before and bits in before:
            value, *waiting = tied(others[0][1], *after)
            others = [(1, value)]
            held += waiting
        own = (place // span) % count
        inside = (place % span) * rows
        merged = jnp.zeros_like(total)
        for mask, value in [(0, total), *others]:
            run = own ^ mask
            gap = jnp.maximum(own - 1 - run, 0) * (span * rows) + inside
            ahead = jnp.exp(-rates * gap.astype(F32)) * value
            entering = entering + jnp.where(run < own, ahead, 0.0)
            gap = (count - 1 - run) * (span * rows)
            merged = merged + jnp.exp(-rates * gap.astype(F32)) * value
        total = merged
    return entering, held


def output_kernel(
    order_ref, added_ref, residual_ref, gain_ref, table_ref, block_ref, packed_ref, logits, squares
):
    at = pl.program_id(0)

    @pl.when(at == 0)
    def _():
        logits[...] = jnp.zeros_like(logits)
        squares[...] = jnp.zeros_like(squares)

    block = (residual_ref[...].astype(F32) + added_ref[0].astype(F32)).astype(BF16)
    block_ref[...] = block
    block_f = block.astype(F32)
    scaled = (block_f * gain_ref[...]).astype(BF16)
    logits[...] += lax.dot_general(
        table_ref[...], scaled, (((1,), (1,)), ((), ())), preferred_element_type=F32
    )
    squared = block_f * block_f
    width = squared.shape[1]
    for start in range(0, width, LANES):
        squares[...] += squared[:, start : start + LANES]

    @pl.when(at == pl.num_programs(0) - 1)
    def _():
        vocab = logits.shape[0]
        summed = jnp.sum(squares[...].T, axis=0, keepdims=True)
        high = summed.astype(BF16).astype(F32)
        row = lax.broadcasted_iota(jnp.int32, (16, summed.shape[1]), 0)
        extra = jnp.where(row == 0, high, jnp.where(row == 1, summed - high, 0.0))
        packed_ref[:vocab, :] = logits[...].astype(BF16)
        packed_ref[vocab:, :] = extra.astype(BF16)


def output_rows(order, added, residual_in, gain, table):
    parts, rows, width = added.shape
    vocab = table.shape[0]
    return pl.pallas_call(
        output_kernel,
        grid_spec=pltpu.PrefetchScalarGridSpec(
            num_scalar_prefetch=1,
            grid=(parts,),
            in_specs=[
                pl.BlockSpec((1, rows, width), lambda p, order: (order[p], 0, 0)),
                pl.BlockSpec((rows, width), lambda p, order: (0, p)),
                pl.BlockSpec((1, width), lambda p, order: (0, p)),
                pl.BlockSpec((vocab, width), lambda p, order: (0, p)),
            ],
            out_specs=[
                pl.BlockSpec((rows, width), lambda p, order: (0, p)),
                pl.BlockSpec((vocab + 16, rows), lambda p, order: (0, 0)),
            ],
            scratch_shapes=[
                pltpu.VMEM((vocab, rows), F32),
                pltpu.VMEM((rows, LANES), F32),
            ],
        ),
        out_shape=[
            jax.ShapeDtypeStruct(residual_in.shape, BF16),
            jax.ShapeDtypeStruct((vocab + 16, rows), BF16),
        ],
        compiler_params=vmem_params(32),
        cost_estimate=pl.CostEstimate(
            flops=2 * rows * parts * width * vocab,
            bytes_accessed=2 * parts * width * (3 * rows + vocab),
            transcendentals=0,
        ),
        name="output_rows",
    )(order, added, residual_in, gain, table)


def like_kernel(width, first_ref, second_ref, ids_ref, like_ref):
    rows = ids_ref.shape[1]
    vocab = first_ref.shape[0] - 16
    total = first_ref[...].astype(F32) + second_ref[...].astype(F32)
    squares = total[vocab : vocab + 1, :] + total[vocab + 1 : vocab + 2, :]
    inv_rms = lax.rsqrt(squares / width + 1e-06)
    logits = total[:vocab, :] * inv_rms
    largest = jnp.max(logits, axis=0, keepdims=True)
    summed = jnp.sum(jnp.exp(logits - largest), axis=0, keepdims=True)
    vocab_ids = lax.broadcasted_iota(jnp.int32, (vocab, rows), 0)
    chosen = jnp.sum(jnp.where(vocab_ids == ids_ref[...], logits, 0.0), axis=0, keepdims=True)
    like_ref[...] = chosen - (largest + jnp.log(summed))


def log_likelihood(first, second, next_ids, width):
    rows = next_ids.shape[0]
    like = pl.pallas_call(
        functools.partial(like_kernel, width),
        out_shape=jax.ShapeDtypeStruct((1, rows), F32),
        compiler_params=pltpu.CompilerParams(vmem_limit_bytes=16 * 1024 * 1024),
        name="log_likelihood",
    )(first, second, next_ids[None, :])
    return like[0]


def summed_over_chan(value):
    count = lax.axis_size("chan")
    total, span = value, 1
    while span < count // 2:
        total = (total.astype(F32) + xor_permute(total, "chan", span).astype(F32)).astype(BF16)
        span *= 2
    return total, xor_permute(total, "chan", span)


def tied(*values):
    return lax.optimization_barrier(values)


def column_pieces(weight, cuts):
    return [lax.slice_in_dim(weight, first, last, axis=1) for first, last in itertools.pairwise(cuts)]


def product(rows, weight):
    return jnp.dot(rows, weight, preferred_element_type=F32).astype(BF16)


def added_up(kept, other):
    return (kept.astype(F32) + other.astype(F32)).astype(BF16)


def placed_permute(value, same, seq_mask, chan_mask):
    count, chans = lax.axis_size("seq"), lax.axis_size("chan")
    pairs = []
    for place, chan in itertools.product(range(count), range(chans)):
        if (place // (count // chans) == chan) == same:
            target = (place ^ seq_mask) * chans + (chan ^ chan_mask)
            pairs.append((place * chans + chan, target))
    return lax.ppermute(value, ("seq", "chan"), pairs)


def projected_fast(gated, out_weight, core_weight, far):
    count, chans = lax.axis_size("seq"), lax.axis_size("chan")
    per_chan = count // chans
    rows, block = gated.shape[0], out_weight.shape[1]
    core, side, low, top = 1, 2, 4, per_chan
    here = lax.axis_index("seq") // per_chan == lax.axis_index("chan")
    part = rows // 2

    halves = [gated[:part], gated[part:]]
    above = [xor_permute(half, "seq", top) for half in halves]
    beside = xor_permute(gated, "seq", side)
    across = [xor_permute(above[0], "seq", side)]
    near = jnp.concatenate([out_weight, core_weight], axis=1)
    first = tied(jnp.concatenate([gated, beside], axis=0))[0]
    near_first = product(first, near)
    across[0], *far = tied(across[0], *far)
    second = [tied(jnp.concatenate([above[0], across[0]], axis=0))[0]]
    far_all = jnp.concatenate(far + [xor_permute(piece, "seq", core) for piece in far], axis=1)

    def first_sums(partial, *after):
        other, *_ = tied(placed_permute(partial, False, 0, 1), *after)
        total = added_up(partial, other)
        return total[:rows], placed_permute(total[rows:], True, side, 0)

    def shared(rows_all):
        close, distant = product(rows_all, near), product(rows_all, far_all)
        return jnp.where(here, distant, close), jnp.where(here, close, distant)

    def second_sums(sent, kept, *after):
        other, *_ = tied(xor_permute(sent, "chan", 1), *after)
        total = added_up(kept, other)
        back = [xor_permute(total[:part], "seq", top), xor_permute(total[part:], "seq", top | side)]
        hop = placed_permute(jnp.concatenate(back, axis=1), True, 0, 1)
        return back, jnp.split(hop, 2, axis=1)

    early = shared(second[0])
    above[1], *_ = tied(above[1], near_first, *early)
    across.append(xor_permute(above[1], "seq", side))
    second.append(tied(jnp.concatenate([above[1], across[1]], axis=0))[0])
    late = shared(second[1])
    sums = [second_sums(*early, late[0]), second_sums(*late)]
    near_sums = first_sums(near_first, across[1])
    far_first, _ = tied(product(first, far_all), late[0])
    far_sums = first_sums(far_first)
    blocks = {}
    for half, mask in itertools.product(range(2), (0, side)):
        span = slice(half * block, (half + 1) * block)
        at = mask // side
        for extra, own, moved in ((0, near_sums, 0), (low, far_sums, 1)):
            late = jnp.concatenate([pair[moved][at][:, span] for pair in sums], axis=0)
            blocks[mask | extra | (half * core)] = jnp.where(here, own[at][:, span], late)
    added = jnp.stack([blocks[mask] for mask in range(per_chan)])
    order = jnp.arange(per_chan, dtype=jnp.int32) ^ (lax.axis_index("seq") % per_chan)
    return added, order


def projected_plain(gated, out_weight):
    count, chans = lax.axis_size("seq"), lax.axis_size("chan")
    per_chan = count // chans
    partial = jnp.dot(
        gated,
        lax.all_gather(out_weight, "seq", axis=1, tiled=True),
        preferred_element_type=F32,
    )
    summed = lax.psum_scatter(partial, "chan", scatter_dimension=1, tiled=True)
    rows = gated.shape[0]
    added = summed.reshape(rows, per_chan, -1).transpose(1, 0, 2)
    return added, jnp.arange(per_chan, dtype=jnp.int32)


def local(
    features,
    residual_in,
    short_filter,
    decay_rates,
    residues,
    skip_gain,
    out_weight,
    final_gain,
    embedding,
    next_ids,
):
    rows, _, width = features.shape
    short_len = short_filter.shape[0]
    modes = decay_rates.shape[1]
    streams = jnp.transpose(features, (1, 0, 2))
    rim = shifted(features[rows - (short_len - 1) :], "seq", 1)
    halo = jnp.pad(
        jnp.transpose(rim, (1, 0, 2)).astype(F32), ((0, 0), (SUBLANES - (short_len - 1), 0), (0, 0))
    )
    taps = short_filter.reshape(short_len * 3, width)
    rates = decay_rates.T.reshape(modes, width // LANES, LANES)
    weights = residues.T.reshape(modes, width // LANES, LANES)
    count, chans = lax.axis_size("seq"), lax.axis_size("chan")
    fast = chans == 2 and count == 16
    top = count // chans
    if fast:
        block = out_weight.shape[1]
        low = top // 2
        far = column_pieces(out_weight, (0, block // 4, block))
        far[0] = xor_permute(far[0], "seq", low)
        core_weight = xor_permute(out_weight, "seq", 1)

    mixed, end = mixed_and_states(streams, halo, taps, rates)
    bits = range(count.bit_length() - 1)
    merges = [(bit,) for bit in bits]
    before = {(2,): far[:1]} if fast else None
    after = far[1:] if fast else ()
    entering, held = entering_states(end, rates, rows, merges, before, after)
    if fast:
        far = held[:1] + [xor_permute(held[1], "seq", low)]
    if fast:
        entering, core_weight = tied(entering, core_weight)
    gated = gated_rows(streams, halo, taps, mixed, skip_gain[None, :], rates, weights, entering)
    if fast:
        added, order = projected_fast(gated, out_weight, core_weight, far)
    else:
        added, order = projected_plain(gated, out_weight)
    block_out, packed = output_rows(order, added, residual_in, final_gain[None, :], embedding)
    first, second = summed_over_chan(packed)
    return block_out, log_likelihood(first, second, next_ids, float(width * chans))


def solution(mesh):
    return jax.shard_map(
        local,
        mesh=mesh,
        in_specs=(
            P("seq", None, "chan"),
            P("seq", "chan"),
            P(None, None, "chan"),
            P("chan", None),
            P("chan", None),
            P("chan"),
            P("chan", "seq"),
            P("chan"),
            P(None, "chan"),
            P("seq"),
        ),
        out_specs=(P("seq", "chan"), P("seq")),
        check_vma=False,
    )
```

```python
import functools
import itertools

import jax
import jax.numpy as jnp
from jax import lax
from jax.experimental import pallas as pl
from jax.experimental.pallas import tpu as pltpu
from jax.sharding import PartitionSpec as P

F32 = jnp.float32
BF16 = jnp.bfloat16
LANES = 128
SUBLANES = 8
GROUP = LANES * SUBLANES


def xor_permute(value, axis, mask):
    count = lax.axis_size(axis)
    return lax.ppermute(value, axis, [(source, source ^ mask) for source in range(count)])


def shifted(value, axis, steps):
    count = lax.axis_size(axis)
    first, last = (max(0, -steps), min(count, count - steps))
    return lax.ppermute(value, axis, [(source, source + steps) for source in range(first, last)])


def fill_stream(scratch, halo, block):
    scratch[:SUBLANES, :] = halo
    scratch[SUBLANES:, :] = block.astype(F32)


def short_stream(scratch, taps_ref, stream, lanes, rows):
    taps = taps_ref.shape[0] // 3
    total = taps_ref[stream : stream + 1, lanes] * scratch[SUBLANES : SUBLANES + rows, lanes]
    for offset in range(1, taps):
        row = offset * 3 + stream
        start = SUBLANES - offset
        total = total + taps_ref[row : row + 1, lanes] * scratch[start : start + rows, lanes]
    return total


def lane_blocks():
    return [(part, slice(part * LANES, (part + 1) * LANES)) for part in range(SUBLANES)]


def states_kernel(
    keys_ref, values_ref, halo_ref, taps_ref, rates_ref, mixed_ref, end_ref, keys_f, values_f, rows_f
):
    rows = mixed_ref.shape[0]
    modes = rates_ref.shape[0]
    fill_stream(keys_f, halo_ref[1], keys_ref[0])
    fill_stream(values_f, halo_ref[2], values_ref[0])
    for part, lanes in lane_blocks():
        mixed = (
            short_stream(keys_f, taps_ref, 1, lanes, rows)
            * short_stream(values_f, taps_ref, 2, lanes, rows)
        ).astype(BF16)
        mixed_ref[:, lanes] = mixed
        rows_f[:, part * SUBLANES : (part + 1) * SUBLANES, :] = mixed.astype(F32).reshape(
            rows // SUBLANES, SUBLANES, LANES
        )
    decay = [jnp.exp(-rates_ref[mode]) for mode in range(modes)]

    def eight(block, states):
        for step in range(SUBLANES):
            entry = rows_f[block, pl.ds(step, SUBLANES, stride=SUBLANES), :]
            states = tuple(d * s + entry for d, s in zip(decay, states))
        return states

    zeros = tuple(jnp.zeros((SUBLANES, LANES), F32) for _ in range(modes))
    states = lax.fori_loop(0, rows // SUBLANES, eight, zeros)
    for mode in range(modes):
        end_ref[mode] = states[mode]


def gated_kernel(
    queries_ref,
    halo_ref,
    taps_ref,
    mixed_ref,
    skip_ref,
    rates_ref,
    residues_ref,
    enter_ref,
    gated_ref,
    queries_f,
    rows_f,
    long_f,
):
    rows = mixed_ref.shape[0]
    modes = rates_ref.shape[0]
    fill_stream(queries_f, halo_ref[0], queries_ref[0])
    for part, lanes in lane_blocks():
        rows_f[:, part * SUBLANES : (part + 1) * SUBLANES, :] = (
            mixed_ref[:, lanes].astype(F32).reshape(rows // SUBLANES, SUBLANES, LANES)
        )
    decay = [jnp.exp(-rates_ref[mode]) for mode in range(modes)]
    weight = [residues_ref[mode] for mode in range(modes)]

    def eight(block, states):
        for step in range(SUBLANES):
            entry = rows_f[block, pl.ds(step, SUBLANES, stride=SUBLANES), :]
            states = tuple(d * s + entry for d, s in zip(decay, states))
            terms = [w * s for w, s in zip(weight, states)]
            while len(terms) > 1:
                terms = [sum(terms[at : at + 2][1:], terms[at]) for at in range(0, len(terms), 2)]
            long_f[block, pl.ds(step, SUBLANES, stride=SUBLANES), :] = terms[0]
        return states

    lax.fori_loop(0, rows // SUBLANES, eight, tuple(enter_ref[mode] for mode in range(modes)))
    for part, lanes in lane_blocks():
        filtered = long_f[:, part * SUBLANES : (part + 1) * SUBLANES, :].reshape(rows, LANES)
        filtered = filtered.astype(BF16).astype(F32)
        direct = skip_ref[:, lanes] * mixed_ref[:, lanes].astype(F32)
        queries = short_stream(queries_f, taps_ref, 0, lanes, rows)
        gated_ref[:, lanes] = (queries * (filtered + direct)).astype(BF16)


def vmem_params(mib):
    return pltpu.CompilerParams(
        dimension_semantics=("arbitrary",), vmem_limit_bytes=mib * 1024 * 1024
    )


def mixed_and_states(streams, halo, taps, rates):
    rows, width = streams.shape[1:]
    modes = rates.shape[0]
    stream = lambda which: pl.BlockSpec((1, rows, GROUP), lambda g: (which, 0, g))
    modal = pl.BlockSpec((modes, SUBLANES, LANES), lambda g: (0, g, 0))
    return pl.pallas_call(
        states_kernel,
        grid=(width // GROUP,),
        in_specs=[
            stream(1),
            stream(2),
            pl.BlockSpec((3, SUBLANES, GROUP), lambda g: (0, 0, g)),
            pl.BlockSpec((taps.shape[0], GROUP), lambda g: (0, g)),
            modal,
        ],
        out_specs=[pl.BlockSpec((rows, GROUP), lambda g: (0, g)), modal],
        out_shape=[
            jax.ShapeDtypeStruct((rows, width), BF16),
            jax.ShapeDtypeStruct(rates.shape, F32),
        ],
        scratch_shapes=[
            pltpu.VMEM((rows + SUBLANES, GROUP), F32),
            pltpu.VMEM((rows + SUBLANES, GROUP), F32),
            pltpu.VMEM((rows // SUBLANES, SUBLANES * SUBLANES, LANES), F32),
        ],
        compiler_params=vmem_params(32),
        cost_estimate=pl.CostEstimate(flops=rows * width, bytes_accessed=rows, transcendentals=0),
        name="mixed_and_states",
    )(streams, streams, halo, taps, rates)


def gated_rows(streams, halo, taps, mixed, skip, rates, residues, entering):
    rows, width = mixed.shape
    modes = rates.shape[0]
    modal = pl.BlockSpec((modes, SUBLANES, LANES), lambda g: (0, g, 0))
    return pl.pallas_call(
        gated_kernel,
        grid=(width // GROUP,),
        in_specs=[
            pl.BlockSpec((1, rows, GROUP), lambda g: (0, 0, g)),
            pl.BlockSpec((3, SUBLANES, GROUP), lambda g: (0, 0, g)),
            pl.BlockSpec((taps.shape[0], GROUP), lambda g: (0, g)),
            pl.BlockSpec((rows, GROUP), lambda g: (0, g)),
            pl.BlockSpec((1, GROUP), lambda g: (0, g)),
            modal,
            modal,
            modal,
        ],
        out_specs=pl.BlockSpec((rows, GROUP), lambda g: (0, g)),
        out_shape=jax.ShapeDtypeStruct((rows, width), BF16),
        scratch_shapes=[
            pltpu.VMEM((rows + SUBLANES, GROUP), F32),
            pltpu.VMEM((rows // SUBLANES, SUBLANES * SUBLANES, LANES), F32),
            pltpu.VMEM((rows // SUBLANES, SUBLANES * SUBLANES, LANES), F32),
        ],
        compiler_params=vmem_params(32),
        cost_estimate=pl.CostEstimate(flops=rows * width, bytes_accessed=rows, transcendentals=0),
        name="gated_rows",
    )(streams, halo, taps, mixed, skip, rates, residues, entering)


def entering_states(end, rates, rows, merges, before=None, after=()):
    place = lax.axis_index("seq")
    total, entering = end, jnp.zeros_like(end)
    held = []
    for bits in merges:
        span, count = 1 << bits[0], 1 << len(bits)
        if before and bits in before:
            total, *held = tied(total, *before[bits])
        others = [
            (mask, xor_permute(total, "seq", mask * span)) for mask in range(1, count)
        ]
        if before and bits in before:
            value, *waiting = tied(others[0][1], *after)
            others = [(1, value)]
            held += waiting
        own = (place // span) % count
        inside = (place % span) * rows
        merged = jnp.zeros_like(total)
        for mask, value in [(0, total), *others]:
            run = own ^ mask
            gap = jnp.maximum(own - 1 - run, 0) * (span * rows) + inside
            ahead = jnp.exp(-rates * gap.astype(F32)) * value
            entering = entering + jnp.where(run < own, ahead, 0.0)
            gap = (count - 1 - run) * (span * rows)
            merged = merged + jnp.exp(-rates * gap.astype(F32)) * value
        total = merged
    return entering, held


def output_kernel(
    order_ref, added_ref, residual_ref, gain_ref, table_ref, block_ref, packed_ref, logits, squares
):
    at = pl.program_id(0)

    @pl.when(at == 0)
    def _():
        logits[...] = jnp.zeros_like(logits)
        squares[...] = jnp.zeros_like(squares)

    block = (residual_ref[...].astype(F32) + added_ref[0].astype(F32)).astype(BF16)
    block_ref[...] = block
    block_f = block.astype(F32)
    scaled = (block_f * gain_ref[...]).astype(BF16)
    logits[...] += lax.dot_general(
        table_ref[...], scaled, (((1,), (1,)), ((), ())), preferred_element_type=F32
    )
    squared = block_f * block_f
    width = squared.shape[1]
    for start in range(0, width, LANES):
        squares[...] += squared[:, start : start + LANES]

    @pl.when(at == pl.num_programs(0) - 1)
    def _():
        vocab = logits.shape[0]
        summed = jnp.sum(squares[...].T, axis=0, keepdims=True)
        high = summed.astype(BF16).astype(F32)
        row = lax.broadcasted_iota(jnp.int32, (16, summed.shape[1]), 0)
        extra = jnp.where(row == 0, high, jnp.where(row == 1, summed - high, 0.0))
        packed_ref[:vocab, :] = logits[...].astype(BF16)
        packed_ref[vocab:, :] = extra.astype(BF16)


def output_rows(order, added, residual_in, gain, table):
    parts, rows, width = added.shape
    vocab = table.shape[0]
    return pl.pallas_call(
        output_kernel,
        grid_spec=pltpu.PrefetchScalarGridSpec(
            num_scalar_prefetch=1,
            grid=(parts,),
            in_specs=[
                pl.BlockSpec((1, rows, width), lambda p, order: (order[p], 0, 0)),
                pl.BlockSpec((rows, width), lambda p, order: (0, p)),
                pl.BlockSpec((1, width), lambda p, order: (0, p)),
                pl.BlockSpec((vocab, width), lambda p, order: (0, p)),
            ],
            out_specs=[
                pl.BlockSpec((rows, width), lambda p, order: (0, p)),
                pl.BlockSpec((vocab + 16, rows), lambda p, order: (0, 0)),
            ],
            scratch_shapes=[
                pltpu.VMEM((vocab, rows), F32),
                pltpu.VMEM((rows, LANES), F32),
            ],
        ),
        out_shape=[
            jax.ShapeDtypeStruct(residual_in.shape, BF16),
            jax.ShapeDtypeStruct((vocab + 16, rows), BF16),
        ],
        compiler_params=vmem_params(32),
        cost_estimate=pl.CostEstimate(
            flops=2 * rows * parts * width * vocab,
            bytes_accessed=2 * parts * width * (3 * rows + vocab),
            transcendentals=0,
        ),
        name="output_rows",
    )(order, added, residual_in, gain, table)


def like_kernel(width, first_ref, second_ref, ids_ref, like_ref):
    rows = ids_ref.shape[1]
    vocab = first_ref.shape[0] - 16
    total = first_ref[...].astype(F32) + second_ref[...].astype(F32)
    squares = total[vocab : vocab + 1, :] + total[vocab + 1 : vocab + 2, :]
    inv_rms = lax.rsqrt(squares / width + 1e-06)
    logits = total[:vocab, :] * inv_rms
    largest = jnp.max(logits, axis=0, keepdims=True)
    summed = jnp.sum(jnp.exp(logits - largest), axis=0, keepdims=True)
    vocab_ids = lax.broadcasted_iota(jnp.int32, (vocab, rows), 0)
    chosen = jnp.sum(jnp.where(vocab_ids == ids_ref[...], logits, 0.0), axis=0, keepdims=True)
    like_ref[...] = chosen - (largest + jnp.log(summed))


def log_likelihood(first, second, next_ids, width):
    rows = next_ids.shape[0]
    like = pl.pallas_call(
        functools.partial(like_kernel, width),
        out_shape=jax.ShapeDtypeStruct((1, rows), F32),
        compiler_params=pltpu.CompilerParams(vmem_limit_bytes=16 * 1024 * 1024),
        name="log_likelihood",
    )(first, second, next_ids[None, :])
    return like[0]


def summed_over_chan(value):
    count = lax.axis_size("chan")
    total, span = value, 1
    while span < count // 2:
        total = (total.astype(F32) + xor_permute(total, "chan", span).astype(F32)).astype(BF16)
        span *= 2
    return total, xor_permute(total, "chan", span)


def tied(*values):
    return lax.optimization_barrier(values)


def column_pieces(weight, cuts):
    return [lax.slice_in_dim(weight, first, last, axis=1) for first, last in itertools.pairwise(cuts)]


def product(rows, weight):
    return jnp.dot(rows, weight, preferred_element_type=F32).astype(BF16)


def added_up(kept, other):
    return (kept.astype(F32) + other.astype(F32)).astype(BF16)


def placed_permute(value, same, seq_mask, chan_mask):
    count, chans = lax.axis_size("seq"), lax.axis_size("chan")
    pairs = []
    for place, chan in itertools.product(range(count), range(chans)):
        if (place // (count // chans) == chan) == same:
            target = (place ^ seq_mask) * chans + (chan ^ chan_mask)
            pairs.append((place * chans + chan, target))
    return lax.ppermute(value, ("seq", "chan"), pairs)


def projected_fast(gated, out_weight, core_weight, far):
    count, chans = lax.axis_size("seq"), lax.axis_size("chan")
    per_chan = count // chans
    rows, block = gated.shape[0], out_weight.shape[1]
    core, side, low, top = 1, 2, 4, per_chan
    here = lax.axis_index("seq") // per_chan == lax.axis_index("chan")
    part = rows // 2

    halves = [gated[:part], gated[part:]]
    above = [xor_permute(half, "seq", top) for half in halves]
    beside = xor_permute(gated, "seq", side)
    across = [xor_permute(above[0], "seq", side)]
    near = jnp.concatenate([out_weight, core_weight], axis=1)
    first = tied(jnp.concatenate([gated, beside], axis=0))[0]
    near_first = product(first, near)
    across[0], *far = tied(across[0], *far)
    second = [tied(jnp.concatenate([above[0], across[0]], axis=0))[0]]
    far_all = jnp.concatenate(far + [xor_permute(piece, "seq", core) for piece in far], axis=1)

    def first_sums(partial, *after):
        other, *_ = tied(placed_permute(partial, False, 0, 1), *after)
        total = added_up(partial, other)
        return total[:rows], placed_permute(total[rows:], True, side, 0)

    def shared(rows_all):
        close, distant = product(rows_all, near), product(rows_all, far_all)
        return jnp.where(here, distant, close), jnp.where(here, close, distant)

    def second_sums(sent, kept, *after):
        other, *_ = tied(xor_permute(sent, "chan", 1), *after)
        total = added_up(kept, other)
        back = [xor_permute(total[:part], "seq", top), xor_permute(total[part:], "seq", top | side)]
        hop = placed_permute(jnp.concatenate(back, axis=1), True, 0, 1)
        return back, jnp.split(hop, 2, axis=1)

    early = shared(second[0])
    above[1], *_ = tied(above[1], near_first, *early)
    across.append(xor_permute(above[1], "seq", side))
    second.append(tied(jnp.concatenate([above[1], across[1]], axis=0))[0])
    late = shared(second[1])
    sums = [second_sums(*early, across[1]), second_sums(*late)]
    near_first, _ = tied(near_first, early[0])
    near_sums = first_sums(near_first, across[1])
    far_first, _ = tied(product(first, far_all), late[0])
    far_sums = first_sums(far_first)
    blocks = {}
    for half, mask in itertools.product(range(2), (0, side)):
        span = slice(half * block, (half + 1) * block)
        at = mask // side
        for extra, own, moved in ((0, near_sums, 0), (low, far_sums, 1)):
            late = jnp.concatenate([pair[moved][at][:, span] for pair in sums], axis=0)
            blocks[mask | extra | (half * core)] = jnp.where(here, own[at][:, span], late)
    added = jnp.stack([blocks[mask] for mask in range(per_chan)])
    order = jnp.arange(per_chan, dtype=jnp.int32) ^ (lax.axis_index("seq") % per_chan)
    return added, order


def projected_plain(gated, out_weight):
    count, chans = lax.axis_size("seq"), lax.axis_size("chan")
    per_chan = count // chans
    partial = jnp.dot(
        gated,
        lax.all_gather(out_weight, "seq", axis=1, tiled=True),
        preferred_element_type=F32,
    )
    summed = lax.psum_scatter(partial, "chan", scatter_dimension=1, tiled=True)
    rows = gated.shape[0]
    added = summed.reshape(rows, per_chan, -1).transpose(1, 0, 2)
    return added, jnp.arange(per_chan, dtype=jnp.int32)


def local(
    features,
    residual_in,
    short_filter,
    decay_rates,
    residues,
    skip_gain,
    out_weight,
    final_gain,
    embedding,
    next_ids,
):
    rows, _, width = features.shape
    short_len = short_filter.shape[0]
    modes = decay_rates.shape[1]
    streams = jnp.transpose(features, (1, 0, 2))
    rim = shifted(features[rows - (short_len - 1) :], "seq", 1)
    halo = jnp.pad(
        jnp.transpose(rim, (1, 0, 2)).astype(F32), ((0, 0), (SUBLANES - (short_len - 1), 0), (0, 0))
    )
    taps = short_filter.reshape(short_len * 3, width)
    rates = decay_rates.T.reshape(modes, width // LANES, LANES)
    weights = residues.T.reshape(modes, width // LANES, LANES)
    count, chans = lax.axis_size("seq"), lax.axis_size("chan")
    fast = chans == 2 and count == 16
    top = count // chans
    if fast:
        block = out_weight.shape[1]
        low = top // 2
        far = column_pieces(out_weight, (0, block // 4, block))
        far[0] = xor_permute(far[0], "seq", low)
        core_weight = xor_permute(out_weight, "seq", 1)

    mixed, end = mixed_and_states(streams, halo, taps, rates)
    bits = range(count.bit_length() - 1)
    merges = [(bit,) for bit in bits]
    before = {(2,): far[:1]} if fast else None
    after = far[1:] if fast else ()
    entering, held = entering_states(end, rates, rows, merges, before, after)
    if fast:
        far = held[:1] + [xor_permute(held[1], "seq", low)]
    if fast:
        entering, core_weight = tied(entering, core_weight)
    gated = gated_rows(streams, halo, taps, mixed, skip_gain[None, :], rates, weights, entering)
    if fast:
        added, order = projected_fast(gated, out_weight, core_weight, far)
    else:
        added, order = projected_plain(gated, out_weight)
    block_out, packed = output_rows(order, added, residual_in, final_gain[None, :], embedding)
    first, second = summed_over_chan(packed)
    return block_out, log_likelihood(first, second, next_ids, float(width * chans))


def solution(mesh):
    return jax.shard_map(
        local,
        mesh=mesh,
        in_specs=(
            P("seq", None, "chan"),
            P("seq", "chan"),
            P(None, None, "chan"),
            P("chan", None),
            P("chan", None),
            P("chan"),
            P("chan", "seq"),
            P("chan"),
            P(None, "chan"),
            P("seq"),
        ),
        out_specs=(P("seq", "chan"), P("seq")),
        check_vma=False,
    )
```

```python
import functools
import itertools

import jax
import jax.numpy as jnp
from jax import lax
from jax.experimental import pallas as pl
from jax.experimental.pallas import tpu as pltpu
from jax.sharding import PartitionSpec as P

F32 = jnp.float32
BF16 = jnp.bfloat16
LANES = 128
SUBLANES = 8
GROUP = LANES * SUBLANES


def xor_permute(value, axis, mask):
    count = lax.axis_size(axis)
    return lax.ppermute(value, axis, [(source, source ^ mask) for source in range(count)])


def shifted(value, axis, steps):
    count = lax.axis_size(axis)
    first, last = (max(0, -steps), min(count, count - steps))
    return lax.ppermute(value, axis, [(source, source + steps) for source in range(first, last)])


def fill_stream(scratch, halo, block):
    scratch[:SUBLANES, :] = halo
    scratch[SUBLANES:, :] = block.astype(F32)


def short_stream(scratch, taps_ref, stream, lanes, rows):
    taps = taps_ref.shape[0] // 3
    total = taps_ref[stream : stream + 1, lanes] * scratch[SUBLANES : SUBLANES + rows, lanes]
    for offset in range(1, taps):
        row = offset * 3 + stream
        start = SUBLANES - offset
        total = total + taps_ref[row : row + 1, lanes] * scratch[start : start + rows, lanes]
    return total


def lane_blocks():
    return [(part, slice(part * LANES, (part + 1) * LANES)) for part in range(SUBLANES)]


def states_kernel(
    keys_ref, values_ref, halo_ref, taps_ref, rates_ref, mixed_ref, end_ref, keys_f, values_f, rows_f
):
    rows = mixed_ref.shape[0]
    modes = rates_ref.shape[0]
    fill_stream(keys_f, halo_ref[1], keys_ref[0])
    fill_stream(values_f, halo_ref[2], values_ref[0])
    for part, lanes in lane_blocks():
        mixed = (
            short_stream(keys_f, taps_ref, 1, lanes, rows)
            * short_stream(values_f, taps_ref, 2, lanes, rows)
        ).astype(BF16)
        mixed_ref[:, lanes] = mixed
        rows_f[:, part * SUBLANES : (part + 1) * SUBLANES, :] = mixed.astype(F32).reshape(
            rows // SUBLANES, SUBLANES, LANES
        )
    decay = [jnp.exp(-rates_ref[mode]) for mode in range(modes)]

    def eight(block, states):
        for step in range(SUBLANES):
            entry = rows_f[block, pl.ds(step, SUBLANES, stride=SUBLANES), :]
            states = tuple(d * s + entry for d, s in zip(decay, states))
        return states

    zeros = tuple(jnp.zeros((SUBLANES, LANES), F32) for _ in range(modes))
    states = lax.fori_loop(0, rows // SUBLANES, eight, zeros)
    for mode in range(modes):
        end_ref[mode] = states[mode]


def gated_kernel(
    queries_ref,
    halo_ref,
    taps_ref,
    mixed_ref,
    skip_ref,
    rates_ref,
    residues_ref,
    enter_ref,
    gated_ref,
    queries_f,
    rows_f,
    long_f,
):
    rows = mixed_ref.shape[0]
    modes = rates_ref.shape[0]
    fill_stream(queries_f, halo_ref[0], queries_ref[0])
    for part, lanes in lane_blocks():
        rows_f[:, part * SUBLANES : (part + 1) * SUBLANES, :] = (
            mixed_ref[:, lanes].astype(F32).reshape(rows // SUBLANES, SUBLANES, LANES)
        )
    decay = [jnp.exp(-rates_ref[mode]) for mode in range(modes)]
    weight = [residues_ref[mode] for mode in range(modes)]

    def eight(block, states):
        for step in range(SUBLANES):
            entry = rows_f[block, pl.ds(step, SUBLANES, stride=SUBLANES), :]
            states = tuple(d * s + entry for d, s in zip(decay, states))
            terms = [w * s for w, s in zip(weight, states)]
            while len(terms) > 1:
                terms = [sum(terms[at : at + 2][1:], terms[at]) for at in range(0, len(terms), 2)]
            long_f[block, pl.ds(step, SUBLANES, stride=SUBLANES), :] = terms[0]
        return states

    lax.fori_loop(0, rows // SUBLANES, eight, tuple(enter_ref[mode] for mode in range(modes)))
    for part, lanes in lane_blocks():
        filtered = long_f[:, part * SUBLANES : (part + 1) * SUBLANES, :].reshape(rows, LANES)
        filtered = filtered.astype(BF16).astype(F32)
        direct = skip_ref[:, lanes] * mixed_ref[:, lanes].astype(F32)
        queries = short_stream(queries_f, taps_ref, 0, lanes, rows)
        gated_ref[:, lanes] = (queries * (filtered + direct)).astype(BF16)


def vmem_params(mib):
    return pltpu.CompilerParams(
        dimension_semantics=("arbitrary",), vmem_limit_bytes=mib * 1024 * 1024
    )


def mixed_and_states(streams, halo, taps, rates):
    rows, width = streams.shape[1:]
    modes = rates.shape[0]
    stream = lambda which: pl.BlockSpec((1, rows, GROUP), lambda g: (which, 0, g))
    modal = pl.BlockSpec((modes, SUBLANES, LANES), lambda g: (0, g, 0))
    return pl.pallas_call(
        states_kernel,
        grid=(width // GROUP,),
        in_specs=[
            stream(1),
            stream(2),
            pl.BlockSpec((3, SUBLANES, GROUP), lambda g: (0, 0, g)),
            pl.BlockSpec((taps.shape[0], GROUP), lambda g: (0, g)),
            modal,
        ],
        out_specs=[pl.BlockSpec((rows, GROUP), lambda g: (0, g)), modal],
        out_shape=[
            jax.ShapeDtypeStruct((rows, width), BF16),
            jax.ShapeDtypeStruct(rates.shape, F32),
        ],
        scratch_shapes=[
            pltpu.VMEM((rows + SUBLANES, GROUP), F32),
            pltpu.VMEM((rows + SUBLANES, GROUP), F32),
            pltpu.VMEM((rows // SUBLANES, SUBLANES * SUBLANES, LANES), F32),
        ],
        compiler_params=vmem_params(32),
        cost_estimate=pl.CostEstimate(flops=rows * width, bytes_accessed=rows, transcendentals=0),
        name="mixed_and_states",
    )(streams, streams, halo, taps, rates)


def gated_rows(streams, halo, taps, mixed, skip, rates, residues, entering):
    rows, width = mixed.shape
    modes = rates.shape[0]
    modal = pl.BlockSpec((modes, SUBLANES, LANES), lambda g: (0, g, 0))
    return pl.pallas_call(
        gated_kernel,
        grid=(width // GROUP,),
        in_specs=[
            pl.BlockSpec((1, rows, GROUP), lambda g: (0, 0, g)),
            pl.BlockSpec((3, SUBLANES, GROUP), lambda g: (0, 0, g)),
            pl.BlockSpec((taps.shape[0], GROUP), lambda g: (0, g)),
            pl.BlockSpec((rows, GROUP), lambda g: (0, g)),
            pl.BlockSpec((1, GROUP), lambda g: (0, g)),
            modal,
            modal,
            modal,
        ],
        out_specs=pl.BlockSpec((rows, GROUP), lambda g: (0, g)),
        out_shape=jax.ShapeDtypeStruct((rows, width), BF16),
        scratch_shapes=[
            pltpu.VMEM((rows + SUBLANES, GROUP), F32),
            pltpu.VMEM((rows // SUBLANES, SUBLANES * SUBLANES, LANES), F32),
            pltpu.VMEM((rows // SUBLANES, SUBLANES * SUBLANES, LANES), F32),
        ],
        compiler_params=vmem_params(32),
        cost_estimate=pl.CostEstimate(flops=rows * width, bytes_accessed=rows, transcendentals=0),
        name="gated_rows",
    )(streams, halo, taps, mixed, skip, rates, residues, entering)


def entering_states(end, rates, rows, merges, before=None, after=()):
    place = lax.axis_index("seq")
    total, entering = end, jnp.zeros_like(end)
    held = []
    for bits in merges:
        span, count = 1 << bits[0], 1 << len(bits)
        if before and bits in before:
            total, *held = tied(total, *before[bits])
        others = [
            (mask, xor_permute(total, "seq", mask * span)) for mask in range(1, count)
        ]
        if before and bits in before:
            value, *waiting = tied(others[0][1], *after)
            others = [(1, value)]
            held += waiting
        own = (place // span) % count
        inside = (place % span) * rows
        merged = jnp.zeros_like(total)
        for mask, value in [(0, total), *others]:
            run = own ^ mask
            gap = jnp.maximum(own - 1 - run, 0) * (span * rows) + inside
            ahead = jnp.exp(-rates * gap.astype(F32)) * value
            entering = entering + jnp.where(run < own, ahead, 0.0)
            gap = (count - 1 - run) * (span * rows)
            merged = merged + jnp.exp(-rates * gap.astype(F32)) * value
        total = merged
    return entering, held


def output_kernel(
    order_ref, added_ref, residual_ref, gain_ref, table_ref, block_ref, packed_ref, logits, squares
):
    at = pl.program_id(0)

    @pl.when(at == 0)
    def _():
        logits[...] = jnp.zeros_like(logits)
        squares[...] = jnp.zeros_like(squares)

    block = (residual_ref[...].astype(F32) + added_ref[0].astype(F32)).astype(BF16)
    block_ref[...] = block
    block_f = block.astype(F32)
    scaled = (block_f * gain_ref[...]).astype(BF16)
    logits[...] += lax.dot_general(
        table_ref[...], scaled, (((1,), (1,)), ((), ())), preferred_element_type=F32
    )
    squared = block_f * block_f
    width = squared.shape[1]
    for start in range(0, width, LANES):
        squares[...] += squared[:, start : start + LANES]

    @pl.when(at == pl.num_programs(0) - 1)
    def _():
        vocab = logits.shape[0]
        summed = jnp.sum(squares[...].T, axis=0, keepdims=True)
        high = summed.astype(BF16).astype(F32)
        row = lax.broadcasted_iota(jnp.int32, (16, summed.shape[1]), 0)
        extra = jnp.where(row == 0, high, jnp.where(row == 1, summed - high, 0.0))
        packed_ref[:vocab, :] = logits[...].astype(BF16)
        packed_ref[vocab:, :] = extra.astype(BF16)


def output_rows(order, added, residual_in, gain, table):
    parts, rows, width = added.shape
    vocab = table.shape[0]
    return pl.pallas_call(
        output_kernel,
        grid_spec=pltpu.PrefetchScalarGridSpec(
            num_scalar_prefetch=1,
            grid=(parts,),
            in_specs=[
                pl.BlockSpec((1, rows, width), lambda p, order: (order[p], 0, 0)),
                pl.BlockSpec((rows, width), lambda p, order: (0, p)),
                pl.BlockSpec((1, width), lambda p, order: (0, p)),
                pl.BlockSpec((vocab, width), lambda p, order: (0, p)),
            ],
            out_specs=[
                pl.BlockSpec((rows, width), lambda p, order: (0, p)),
                pl.BlockSpec((vocab + 16, rows), lambda p, order: (0, 0)),
            ],
            scratch_shapes=[
                pltpu.VMEM((vocab, rows), F32),
                pltpu.VMEM((rows, LANES), F32),
            ],
        ),
        out_shape=[
            jax.ShapeDtypeStruct(residual_in.shape, BF16),
            jax.ShapeDtypeStruct((vocab + 16, rows), BF16),
        ],
        compiler_params=vmem_params(32),
        cost_estimate=pl.CostEstimate(
            flops=2 * rows * parts * width * vocab,
            bytes_accessed=2 * parts * width * (3 * rows + vocab),
            transcendentals=0,
        ),
        name="output_rows",
    )(order, added, residual_in, gain, table)


def like_kernel(width, first_ref, second_ref, ids_ref, like_ref):
    rows = ids_ref.shape[1]
    vocab = first_ref.shape[0] - 16
    total = first_ref[...].astype(F32) + second_ref[...].astype(F32)
    squares = total[vocab : vocab + 1, :] + total[vocab + 1 : vocab + 2, :]
    inv_rms = lax.rsqrt(squares / width + 1e-06)
    logits = total[:vocab, :] * inv_rms
    largest = jnp.max(logits, axis=0, keepdims=True)
    summed = jnp.sum(jnp.exp(logits - largest), axis=0, keepdims=True)
    vocab_ids = lax.broadcasted_iota(jnp.int32, (vocab, rows), 0)
    chosen = jnp.sum(jnp.where(vocab_ids == ids_ref[...], logits, 0.0), axis=0, keepdims=True)
    like_ref[...] = chosen - (largest + jnp.log(summed))


def log_likelihood(first, second, next_ids, width):
    rows = next_ids.shape[0]
    like = pl.pallas_call(
        functools.partial(like_kernel, width),
        out_shape=jax.ShapeDtypeStruct((1, rows), F32),
        compiler_params=pltpu.CompilerParams(vmem_limit_bytes=16 * 1024 * 1024),
        name="log_likelihood",
    )(first, second, next_ids[None, :])
    return like[0]


def summed_over_chan(value):
    count = lax.axis_size("chan")
    total, span = value, 1
    while span < count // 2:
        total = (total.astype(F32) + xor_permute(total, "chan", span).astype(F32)).astype(BF16)
        span *= 2
    return total, xor_permute(total, "chan", span)


def tied(*values):
    return lax.optimization_barrier(values)


def column_pieces(weight, cuts):
    return [lax.slice_in_dim(weight, first, last, axis=1) for first, last in itertools.pairwise(cuts)]


def product(rows, weight):
    return jnp.dot(rows, weight, preferred_element_type=F32).astype(BF16)


def added_up(kept, other):
    return (kept.astype(F32) + other.astype(F32)).astype(BF16)


def placed_permute(value, same, seq_mask, chan_mask):
    count, chans = lax.axis_size("seq"), lax.axis_size("chan")
    pairs = []
    for place, chan in itertools.product(range(count), range(chans)):
        if (place // (count // chans) == chan) == same:
            target = (place ^ seq_mask) * chans + (chan ^ chan_mask)
            pairs.append((place * chans + chan, target))
    return lax.ppermute(value, ("seq", "chan"), pairs)


def projected_fast(gated, out_weight, core_weight, far):
    count, chans = lax.axis_size("seq"), lax.axis_size("chan")
    per_chan = count // chans
    rows, block = gated.shape[0], out_weight.shape[1]
    core, side, low, top = 1, 2, 4, per_chan
    here = lax.axis_index("seq") // per_chan == lax.axis_index("chan")
    part = rows // 2

    halves = [gated[:part], gated[part:]]
    above = [xor_permute(half, "seq", top) for half in halves]
    beside = xor_permute(gated, "seq", side)
    across = [xor_permute(above[0], "seq", side)]
    near = jnp.concatenate([out_weight, core_weight], axis=1)
    first = tied(jnp.concatenate([gated, beside], axis=0))[0]
    across[0], *far = tied(across[0], *far)
    second = [tied(jnp.concatenate([above[0], across[0]], axis=0))[0]]
    far_all = jnp.concatenate(far + [xor_permute(piece, "seq", core) for piece in far], axis=1)

    def first_sums(partial, *after):
        other, *_ = tied(placed_permute(partial, False, 0, 1), *after)
        total = added_up(partial, other)
        return total[:rows], placed_permute(total[rows:], True, side, 0)

    def shared(rows_all):
        close, distant = product(rows_all, near), product(rows_all, far_all)
        return jnp.where(here, distant, close), jnp.where(here, close, distant)

    def second_sums(sent, kept, *after):
        other, *_ = tied(xor_permute(sent, "chan", 1), *after)
        total = added_up(kept, other)
        back = [xor_permute(total[:part], "seq", top), xor_permute(total[part:], "seq", top | side)]
        hop = placed_permute(jnp.concatenate(back, axis=1), True, 0, 1)
        return back, jnp.split(hop, 2, axis=1)

    early = shared(second[0])
    above[1], *_ = tied(above[1], *early)
    across.append(xor_permute(above[1], "seq", side))
    second.append(tied(jnp.concatenate([above[1], across[1]], axis=0))[0])
    late = shared(second[1])
    sums = [second_sums(*early, across[1]), second_sums(*late)]
    near_first = product(tied(first, early[0])[0], near)
    near_sums = first_sums(near_first, across[1])
    far_first, _ = tied(product(first, far_all), late[0])
    far_sums = first_sums(far_first)
    blocks = {}
    for half, mask in itertools.product(range(2), (0, side)):
        span = slice(half * block, (half + 1) * block)
        at = mask // side
        for extra, own, moved in ((0, near_sums, 0), (low, far_sums, 1)):
            late = jnp.concatenate([pair[moved][at][:, span] for pair in sums], axis=0)
            blocks[mask | extra | (half * core)] = jnp.where(here, own[at][:, span], late)
    added = jnp.stack([blocks[mask] for mask in range(per_chan)])
    order = jnp.arange(per_chan, dtype=jnp.int32) ^ (lax.axis_index("seq") % per_chan)
    return added, order


def projected_plain(gated, out_weight):
    count, chans = lax.axis_size("seq"), lax.axis_size("chan")
    per_chan = count // chans
    partial = jnp.dot(
        gated,
        lax.all_gather(out_weight, "seq", axis=1, tiled=True),
        preferred_element_type=F32,
    )
    summed = lax.psum_scatter(partial, "chan", scatter_dimension=1, tiled=True)
    rows = gated.shape[0]
    added = summed.reshape(rows, per_chan, -1).transpose(1, 0, 2)
    return added, jnp.arange(per_chan, dtype=jnp.int32)


def local(
    features,
    residual_in,
    short_filter,
    decay_rates,
    residues,
    skip_gain,
    out_weight,
    final_gain,
    embedding,
    next_ids,
):
    rows, _, width = features.shape
    short_len = short_filter.shape[0]
    modes = decay_rates.shape[1]
    streams = jnp.transpose(features, (1, 0, 2))
    rim = shifted(features[rows - (short_len - 1) :], "seq", 1)
    halo = jnp.pad(
        jnp.transpose(rim, (1, 0, 2)).astype(F32), ((0, 0), (SUBLANES - (short_len - 1), 0), (0, 0))
    )
    taps = short_filter.reshape(short_len * 3, width)
    rates = decay_rates.T.reshape(modes, width // LANES, LANES)
    weights = residues.T.reshape(modes, width // LANES, LANES)
    count, chans = lax.axis_size("seq"), lax.axis_size("chan")
    fast = chans == 2 and count == 16
    top = count // chans
    if fast:
        block = out_weight.shape[1]
        low = top // 2
        far = column_pieces(out_weight, (0, block // 4, block))
        far[0] = xor_permute(far[0], "seq", low)
        core_weight = xor_permute(out_weight, "seq", 1)

    mixed, end = mixed_and_states(streams, halo, taps, rates)
    bits = range(count.bit_length() - 1)
    merges = [(bit,) for bit in bits]
    before = {(2,): far[:1]} if fast else None
    after = far[1:] if fast else ()
    entering, held = entering_states(end, rates, rows, merges, before, after)
    if fast:
        far = held[:1] + [xor_permute(held[1], "seq", low)]
    if fast:
        entering, core_weight = tied(entering, core_weight)
    gated = gated_rows(streams, halo, taps, mixed, skip_gain[None, :], rates, weights, entering)
    if fast:
        added, order = projected_fast(gated, out_weight, core_weight, far)
    else:
        added, order = projected_plain(gated, out_weight)
    block_out, packed = output_rows(order, added, residual_in, final_gain[None, :], embedding)
    first, second = summed_over_chan(packed)
    return block_out, log_likelihood(first, second, next_ids, float(width * chans))


def solution(mesh):
    return jax.shard_map(
        local,
        mesh=mesh,
        in_specs=(
            P("seq", None, "chan"),
            P("seq", "chan"),
            P(None, None, "chan"),
            P("chan", None),
            P("chan", None),
            P("chan"),
            P("chan", "seq"),
            P("chan"),
            P(None, "chan"),
            P("seq"),
        ),
        out_specs=(P("seq", "chan"), P("seq")),
        check_vma=False,
    )
```
